32 devices in a mesh: seq: 8 (over z, y), head: 4 (over x, core).
Axes of the slice: x: 2, y: 2, z: 4, core: 2. Of those that a mesh axis runs over, the one named last changes fastest.
Arguments:
- tokens: bfloat16 [14112, 384], P(('seq', 'head')), may hold values from -6 to 6
- actions: bfloat16 [24, 3, 384], P('seq'), may hold values from -6 to 6
- action_mask: int32 [24, 3], P('seq'), may hold values 0 or 1
- frame_mask: int32 [24, 3, 3], P('seq'), may hold values from 0 to 1, as said below
- environment_id: int32 [24], P('seq'), may hold values from 0 to 7
- environment_embed: float32 [8, 384], replicated, may hold values from -3 to 3
- norm_gain: float32 [2, 2, 384], replicated, may hold values from 0.25 to 1.75
- norm_bias: float32 [2, 2, 384], replicated, may hold values from -2 to 2
- input_weight: bfloat16 [2, 3, 384, 1024], P(None, None, None, 'head'), may hold values from -0.3125 to 0.3125
- output_weight: bfloat16 [2, 1024, 384], P(None, 'head'), may hold values from -1.5 to 1.5
- output_bias: float32 [2, 384], replicated, may hold values from -2 to 2
- up_weight: bfloat16 [2, 384, 2048], replicated, may hold values from -0.3125 to 0.3125
- up_bias: float32 [2, 2048], replicated, may hold values from -3 to 3
- down_weight: bfloat16 [2, 2048, 384], replicated, may hold values from -0.25 to 0.25
- down_bias: float32 [2, 384], replicated, may hold values from -2 to 2
- cotangent: bfloat16 [14112, 384], P(('seq', 'head')), may hold values from -6 to 6
Outputs:
- mixed: bfloat16 [14112, 384], P(('seq', 'head'))
- tokens_gradient: float32 [14112, 384], P(('seq', 'head'))
- environment_gradient: float32 [8, 384], replicated
- gain_gradient: float32 [2, 2, 384], replicated
- bias_gradient: float32 [2, 2, 384], replicated
- input_weight_gradient: float32 [2, 3, 384, 1024], P(None, None, None, 'head')
- output_weight_gradient: float32 [2, 1024, 384], P(None, 'head')
- output_bias_gradient: float32 [2, 384], replicated
- up_weight_gradient: float32 [2, 384, 2048], replicated
- up_bias_gradient: float32 [2, 2048], replicated
- down_weight_gradient: float32 [2, 2048, 384], replicated
- down_bias_gradient: float32 [2, 384], replicated
The draws below stay inside these ranges and needn't reach their ends.
Inputs may be any that keep to these rules, and one draw needn't show every extreme that they name: frame_mask[s, f, f] = 1 and frame_mask[s, f, g] = 0 for g > f: a frame never reads a later one and always reads itself; earlier frames may be hidden.
All inputs are finite; a program needn't handle non-finite values. No bound on the sum of `action_mask` on one device may be relied on, other than what follows from the above.
Results may differ from the reference program's by a relative error of at most 0.018.
Values may be sent and summed in bfloat16 or wider, within the bound.
No kernel may reach another device: no remote copies, remote signals or barrier semaphores. Data moves between devices by JAX's collectives and lax.ppermute only.
A program may use at most 192 MiB of HBM per device.

```python
from functools import partial
import jax
import jax.numpy as jnp
from jax import lax

D = 384
HEADS = 16
HEAD_DIM = 64
FF = 2048
FRAMES = 3
PATCHES = 196
LAYERS = 2
ENVS = 8
INNER = 1024
TOKS = 588
SEQS = 24
ROWS = 14112


def draw_frame_mask(key, part):
    key = jax.random.fold_in(key, 7)
    coins = jax.random.randint(key, (SEQS, FRAMES, FRAMES), 0, 2)
    row_index = jnp.arange(FRAMES)[:, None]
    col_index = jnp.arange(FRAMES)[None, :]
    picked = jnp.where(col_index < row_index, coins, 0)
    return jnp.where(col_index == row_index, 1, picked).astype(jnp.int32)


def with_ends(values, stream_key, least, high):
    longest = values.shape.index(max(values.shape))
    spots = []
    for shift in (0, 1):
        where = [jax.random.randint(jax.random.fold_in(stream_key, axis), (), 0, length) for axis, length in enumerate(values.shape)]
        where[longest] = (where[longest] + shift) % values.shape[longest]
        spots.append(tuple(where))
    return values.at[spots[0]].set(least).at[spots[1]].set(high)


def levels(stream_key, shape, split, least, largest):
    loudness = 1.0
    for axis_at, blocks in split:
        draws = jax.random.uniform(jax.random.fold_in(jax.random.fold_in(stream_key, 6), axis_at), (blocks,), jnp.float32, least / len(split), largest / len(split))
        loudness = loudness * jnp.repeat(jnp.exp(draws), shape[axis_at] // blocks).reshape((-1,) + (1,) * (len(shape) - 1 - axis_at))
    return loudness


def normal_values(stream_key, shape, scale, bound, pieces=(), dtype=jnp.bfloat16):
    level = levels(stream_key, shape, pieces, -0.22, 0.18) if pieces else 1.0
    values = jax.random.normal(stream_key, shape, jnp.float32) * scale * level
    return jnp.minimum(jnp.maximum(values, -bound), bound).astype(dtype)


def setup_inputs(seed: int = 0) -> dict:
    arg_keys = jax.random.split(jax.random.key(seed), 17)
    return {
        "tokens": normal_values(arg_keys[0], (ROWS, D), 1.0, 6.0, ((0, 32),)),
        "actions": normal_values(arg_keys[1], (SEQS, FRAMES, D), 1.0, 6.0, ((0, 8),)),
        "action_mask": with_ends((jax.random.randint(arg_keys[2], (SEQS, FRAMES), 0, 4) < 3).astype(jnp.int32), jax.random.fold_in(arg_keys[2], 1), 0, 1),
        "frame_mask": draw_frame_mask(jax.random.fold_in(arg_keys[16], 71), 0),
        "environment_id": with_ends(jax.random.randint(arg_keys[4], (SEQS,), 0, ENVS), jax.random.fold_in(arg_keys[4], 1), 0, ENVS - 1).astype(jnp.int32),
        "environment_embed": normal_values(arg_keys[5], (ENVS, D), 0.5, 3.0, (), jnp.float32),
        "norm_gain": jnp.clip(1.0 + 0.15 * jax.random.normal(arg_keys[6], (LAYERS, 2, D), jnp.float32), 0.25, 1.75),
        "norm_bias": normal_values(arg_keys[7], (LAYERS, 2, D), 0.3, 2.0, (), jnp.float32),
        "input_weight": normal_values(arg_keys[8], (LAYERS, 3, D, INNER), D ** -0.5, 0.3125, ((3, 4),)),
        "output_weight": normal_values(arg_keys[9], (LAYERS, INNER, D), (INNER // 64) ** -0.5, 1.5, ((1, 4),)),
        "output_bias": normal_values(arg_keys[10], (LAYERS, D), 0.3, 2.0, (), jnp.float32),
        "up_weight": normal_values(arg_keys[11], (LAYERS, D, FF), D ** -0.5, 0.3125),
        "up_bias": normal_values(arg_keys[12], (LAYERS, FF), 0.5, 3.0, (), jnp.float32),
        "down_weight": normal_values(arg_keys[13], (LAYERS, FF, D), (FF // 4) ** -0.5, 0.25),
        "down_bias": normal_values(arg_keys[14], (LAYERS, D), 0.3, 2.0, (), jnp.float32),
        "cotangent": normal_values(arg_keys[15], (ROWS, D), 1.0, 6.0, ((0, 32),)),
    }


EPSILON = 1e-05
MASKED = -1e+30
EXACT = lax.Precision.HIGHEST

@jax.custom_vjp
def low(v):
    return lax.optimization_barrier(v.astype(jnp.bfloat16)).astype(jnp.float32)

@jax.custom_vjp
def low_back(v):
    return v

def low_keep(v):
    return (low(v), None)

def low_pass(kept, grad):
    return (grad,)

def back_keep(v):
    return (v, None)

def back_low(kept, grad):
    return (low(grad),)
low.defvjp(low_keep, low_pass)
low_back.defvjp(back_keep, back_low)

def norm_apply(values, gain, shift):
    center = values - lax.optimization_barrier(jnp.mean(values, axis=-1, keepdims=True))
    spread = lax.optimization_barrier(jnp.mean(center * center, axis=-1, keepdims=True))
    return center * lax.rsqrt(spread + EPSILON) * gain + shift

def attend(item):
    queries, keys, values, frames = item
    allowed = jnp.repeat(jnp.repeat(frames, PATCHES, 0), PATCHES, 1) > 0
    scores = jnp.einsum('ahe,bhe->hab', queries, keys, precision=EXACT) * HEAD_DIM ** (-0.5)
    scores = jnp.where(allowed[None], low_back(scores), MASKED)
    weights = low(jax.nn.softmax(scores, axis=-1))
    blended = jnp.einsum('hab,bhe->ahe', weights, values, precision=EXACT)
    return low(low_back(blended.reshape(TOKS, INNER)))

def forward(acted, frame_mask, environment_id, tokens, environment_embed, norm_gain, norm_bias, input_weight, output_weight, output_bias, up_weight, up_bias, down_weight, down_bias):
    chosen = (environment_id[:, None] == jnp.arange(ENVS)[None, :]).astype(jnp.float32)
    condition = acted + jnp.dot(chosen, environment_embed, precision=EXACT)[:, None, :]
    condition = jnp.broadcast_to(condition[:, :, None, :], (SEQS, FRAMES, PATCHES, D)).reshape(ROWS, D)
    stream = tokens + condition
    for layer_index in range(LAYERS):
        normed = low(norm_apply(stream, norm_gain[layer_index, 0], norm_bias[layer_index, 0]))
        triple = jnp.einsum('rd,tde->tre', normed, input_weight[layer_index], precision=EXACT)
        triple = low(low_back(triple)).reshape(3, SEQS, TOKS, HEADS, HEAD_DIM)
        attention = lax.map(jax.checkpoint(attend), (triple[0], triple[1], triple[2], frame_mask))
        attention = attention.reshape(ROWS, INNER)
        projected = low_back(jnp.dot(attention, output_weight[layer_index], precision=EXACT))
        stream = stream + (projected + output_bias[layer_index])
        lifted = low(norm_apply(stream, norm_gain[layer_index, 1], norm_bias[layer_index, 1]))
        before = low_back(jnp.dot(lifted, up_weight[layer_index], precision=EXACT)) + up_bias[layer_index]
        hidden = low(jax.nn.gelu(before, approximate=False))
        lowered = low_back(jnp.dot(hidden, down_weight[layer_index], precision=EXACT))
        stream = stream + (lowered + down_bias[layer_index])
    return stream

def reference(tokens, actions, action_mask, frame_mask, environment_id, environment_embed, norm_gain, norm_bias, input_weight, output_weight, output_bias, up_weight, up_bias, down_weight, down_bias, cotangent):
    acted = actions.astype(jnp.float32) * action_mask[:, :, None].astype(jnp.float32)
    primals = (tokens.astype(jnp.float32), environment_embed, norm_gain, norm_bias, input_weight.astype(jnp.float32), output_weight.astype(jnp.float32), output_bias, up_weight.astype(jnp.float32), up_bias, down_weight.astype(jnp.float32), down_bias)
    result, pullback = jax.vjp(partial(forward, acted, frame_mask, environment_id), *primals)
    grads = pullback(cotangent.astype(jnp.float32))
    return (result.astype(jnp.bfloat16), grads[0], grads[1], grads[2], grads[3], grads[4], grads[5], grads[6], grads[7], grads[8], grads[9], grads[10])
```

```python
import functools
import math

import jax
import jax.numpy as jnp
from jax import lax
from jax.experimental import pallas as pl
from jax.experimental.pallas import tpu as pltpu
from jax.sharding import PartitionSpec as P

HEAD_DIM = 64
EPSILON = 1e-05
MASKED = -1e30
LOG2E = math.log2(math.e)
LN2 = math.log(2.0)
LANES = 128
BF16 = jnp.bfloat16
F32 = jnp.float32
NT = (((1,), (1,)), ((), ()))
NN = (((1,), (0,)), ((), ()))
TN = (((0,), (0,)), ((), ()))
MIB = 1024 * 1024
SMEM = pltpu.MemorySpace.SMEM


def up_to(value, step):
    return -(-value // step) * step


def dot(a, b, dims=NN):
    return lax.dot_general(a, b, dims, preferred_element_type=F32)


class Plan:
    def __init__(self, rows, groups, seqs, frames, width, local_width, hidden):
        self.rows, self.groups, self.seqs, self.frames = rows, groups, seqs, frames
        self.width, self.local, self.hidden = width, local_width, hidden
        self.block = up_to(rows, 16)
        self.total = self.block * groups
        self.length = rows * groups // seqs
        self.patches = self.length // frames
        self.heads = local_width // HEAD_DIM
        self.group_lanes = LANES // self.heads
        place = lambda t: t // rows * self.block + t % rows
        starts = [place(s * self.length) // 16 * 16 for s in range(seqs)]
        ends = [place((s + 1) * self.length - 1) + 1 for s in range(seqs)]
        self.window = max(up_to(e - s, 16) for s, e in zip(starts, ends))
        self.stride = starts[1] - starts[0]
        assert seqs == 3 and groups == 4
        assert starts == [self.stride * s for s in range(seqs)]
        assert self.window <= 2 * self.block
        assert starts[-1] + self.window <= self.total
        self.lanes = up_to(self.window, LANES)
        first = [
            min(place(s * self.length + f * self.patches) - starts[s] for s in range(seqs))
            for f in range(frames)
        ]
        last = [
            max(
                place(s * self.length + (f + 1) * self.patches - 1) - starts[s] + 1
                for s in range(seqs)
            )
            for f in range(frames)
        ]
        self.cuts = [first[f] // 16 * 16 if f else 0 for f in range(frames)] + [self.window]
        ends = [0] + [min(up_to(last[f], LANES), self.lanes) for f in range(frames - 1)] + [self.lanes]
        self.key_chunks = [
            (ends[f], ends[f + 1] - ends[f], self.cuts[f]) for f in range(frames)
        ]
        begins = [first[f] // LANES * LANES if f else 0 for f in range(frames)] + [self.lanes]
        reach = [up_to(last[f], 16) for f in range(frames - 1)] + [self.window]
        self.query_chunks = [
            (begins[f], begins[f + 1] - begins[f], reach[f]) for f in range(frames)
        ]

    def sequence(self, slot, across):
        if slot == 2:
            return 1
        return across * (self.seqs - 1) if slot == 0 else (1 - across) * (self.seqs - 1)


def params(mib):
    return pltpu.CompilerParams(vmem_limit_bytes=mib * MIB)


def result(shape, dtype, away=False):
    return pltpu.HBM(shape, dtype) if away else jax.ShapeDtypeStruct(shape, dtype)


def far(arrays, away=True):
    return [pltpu.with_memory_space_constraint(a, pltpu.HBM) if away else a for a in arrays]


def cost(microseconds):
    return pl.CostEstimate(flops=0, bytes_accessed=int(3.69e6 * microseconds), transcendentals=0)


def full(shape):
    return pl.BlockSpec(shape, lambda *i: (0,) * len(shape))


def layer_of(shape, layer):
    return pl.BlockSpec((None,) + shape, lambda *i: (layer,) + (0,) * len(shape))


def norm_stats(values):
    center = values - jnp.mean(values, axis=-1, keepdims=True)
    spread = jnp.mean(center * center, axis=-1, keepdims=True)
    return center, lax.rsqrt(spread + EPSILON)


def norm_back(upstream, center, scale, gain):
    unit = center * scale
    weighted = upstream * gain
    mean_w = jnp.mean(weighted, axis=-1, keepdims=True)
    mean_wn = jnp.mean(weighted * unit, axis=-1, keepdims=True)
    grad = scale * (weighted - mean_w - unit * mean_wn)
    return (
        grad,
        jnp.sum(upstream * unit, axis=0, keepdims=True),
        jnp.sum(upstream, axis=0, keepdims=True),
    )


def prologue_kernel(
    plan, me_ref, act_mask, frame_mask, env_id, tokens, actions, embed, gain, shift, stream, normed, qhot, kbias, valid
):
    rows, block = plan.rows, plan.block
    row = lax.broadcasted_iota(jnp.int32, (block, plan.width), 0)
    place = me_ref[0] * rows + row
    condition = jnp.zeros((block, plan.width), F32)
    for s in range(plan.seqs):
        env = jnp.zeros((1, plan.width), F32)
        for e in range(embed.shape[0]):
            env = jnp.where(env_id[0:1, s : s + 1] == e, embed[e : e + 1, :], env)
        for f in range(plan.frames):
            mask = act_mask[s : s + 1, f : f + 1].astype(F32)
            term = actions[s, f : f + 1, :].astype(F32) * mask + env
            begin = s * plan.length + f * plan.patches
            condition = jnp.where(
                (place >= begin) & (place < begin + plan.patches), term, condition
            )
    padded = jnp.concatenate(
        [tokens[...].astype(F32), jnp.zeros((block - rows, plan.width), F32)], axis=0
    )
    values = jnp.where(row < rows, padded + condition, 0.0)
    stream[...] = values
    center, scale = norm_stats(values)
    normed[...] = (center * scale * gain[0:1, :] + shift[0:1, :]).astype(BF16)
    line = lax.broadcasted_iota(jnp.int32, (plan.lanes, LANES), 0)
    lane = lax.broadcasted_iota(jnp.int32, (plan.lanes, LANES), 1) % plan.group_lanes
    for slot in range(plan.seqs):
        s = plan.sequence(slot, me_ref[0] // 2)
        at = plan.stride * s + line
        origin = at
        inside = line < plan.window
        for b in range(plan.groups):
            here = (at >= b * block) & (at < (b + 1) * block)
            origin = jnp.where(here, at - b * (block - rows), origin)
            inside = inside & jnp.logical_not(here & (at >= b * block + rows))
        token = origin - s * plan.length
        inside = inside & (token >= 0) & (token < plan.length)
        frame = jnp.zeros_like(token)
        for f in range(1, plan.frames):
            frame = frame + jnp.where(token >= f * plan.patches, 1, 0)
        frame = jnp.where(inside, frame, -1)
        qhot[slot] = jnp.where((lane == frame) & inside, 1.0, 0.0).astype(BF16)
        valid[slot] = jnp.where(inside, 1.0, 0.0)[: plan.window].astype(BF16)
        bias = jnp.where(lane < plan.frames, MASKED, 0.0)
        bias = jnp.where((lane >= plan.frames) & (lane < plan.frames + 3), 1.0, bias)
        allowed = frame_mask[s]
        for f in range(plan.frames):
            for g in range(plan.frames):
                value = jnp.where(allowed[f : f + 1, g : g + 1] > 0, 0.0, MASKED)
                bias = jnp.where((lane == f) & (frame == g), value, bias)
        kbias[slot] = bias.astype(BF16)


def prologue(plan, me, action_mask, frame_mask, env_id, tokens, actions, embed, gain, shift):
    return pl.pallas_call(
        functools.partial(prologue_kernel, plan),
        grid=(1,),
        in_specs=[pl.BlockSpec(memory_space=SMEM)]
        + [full(action_mask.shape), full(frame_mask.shape), full(env_id.shape)]
        + [full(tokens.shape), full(actions.shape), full(embed.shape)]
        + [layer_of(gain.shape[1:], 0), layer_of(gain.shape[1:], 0)],
        out_specs=[
            full((plan.block, plan.width)),
            full((plan.block, plan.width)),
            full((plan.seqs, plan.lanes, LANES)),
            full((plan.seqs, plan.lanes, LANES)),
            full((plan.seqs, plan.window, LANES)),
        ],
        out_shape=[
            jax.ShapeDtypeStruct((plan.block, plan.width), F32),
            jax.ShapeDtypeStruct((plan.block, plan.width), BF16),
            result((plan.seqs, plan.lanes, LANES), BF16),
            result((plan.seqs, plan.lanes, LANES), BF16),
            result((plan.seqs, plan.window, LANES), BF16),
        ],
        compiler_params=params(16),
        cost_estimate=cost(5),
        name="prologue",
    )(me, *far([action_mask, frame_mask, env_id, tokens, actions, embed, gain, shift]))


def place_blocks(plan, me, blocks, target):
    x, c = me[0] // 2, me[0] % 2
    if len(blocks) == 2:
        order = [c, 1 - c]
    else:
        order = [2 * x + c, 2 * x + 1 - c, 2 * (1 - x) + c, 2 * (1 - x) + 1 - c]
    for ref, b in zip(blocks, order):
        target[pl.ds(pl.multiple_of(b * plan.block, 16), plan.block), :] = ref[...]


def scatter_blocks(plan, me, block_of, outs):
    x, c = me[0] // 2, me[0] % 2
    order = [2 * (1 - x) + 1 - c, 2 * x + 1 - c, 2 * (1 - x) + c, 2 * x + c]
    for ref, b in zip(outs, order):
        rows = pl.ds(pl.multiple_of(b * plan.block, 16), plan.block)
        ref[...] = block_of(rows).astype(BF16)


def window_start(plan, me, slots, blocks):
    x = me[0] // 2
    if len(slots) == 1:
        s = plan.sequence(slots[0], x)
    else:
        s = jnp.int32(0)
        for i, slot in enumerate(slots):
            s = jnp.where(pl.program_id(0) == i, plan.sequence(slot, x), s)
    start = s * plan.stride
    if blocks == 2:
        start = start - x * (2 * plan.block)
    return pl.multiple_of(start, 16)


def group_mask(plan, head):
    lane = lax.broadcasted_iota(jnp.int32, (1, LANES), 1)
    return jnp.where(lane // plan.group_lanes == head, 1.0, 0.0).astype(BF16)


def put_windows(plan, me, slots, before, target, value):
    over = plan.window - plan.stride
    step = pl.program_id(0)
    at = window_start(plan, me, slots, 4)

    @pl.when(step == 0)
    def _():
        target[...] = jnp.zeros(target.shape, target.dtype)
        for slot, ref in enumerate(before):
            start = pl.multiple_of(plan.sequence(slot, me[0] // 2) * plan.stride, 16)
            target[pl.ds(start, plan.window), :] = ref[0]

    inner = pl.ds(pl.multiple_of(at + over, 16), plan.window - 2 * over)
    target[inner, :] = value[over : plan.window - over]
    for begin in (0, plan.window - over):
        rows = pl.ds(pl.multiple_of(at + begin, 16), over)
        target[rows, :] = target[rows, :] + value[begin : begin + over]


def attend_kernel(plan, slots, blocks, *refs):
    me, refs = refs[0], refs[1:]
    placed, refs = refs[:blocks], refs[blocks:]
    w_in, qhot, kbias, valid = refs[:4]
    refs = refs[4:]
    last = blocks == 4
    if last:
        w_out, before, refs = refs[0], refs[1], refs[2:]
    triple, attention, lse = refs[:3]
    refs = refs[3:]
    if last:
        outs, refs = refs[:4], refs[4:]
    gathered, q_even, q_odd, keys, values, *whole = refs
    window, local = plan.window, plan.local

    @pl.when(pl.program_id(0) == 0)
    def _():
        place_blocks(plan, me, placed, gathered)
        keys[window:, :] = jnp.zeros((plan.lanes - window, local), BF16)
        values[window:, :] = jnp.zeros((plan.lanes - window, local), BF16)

    x = gathered[pl.ds(window_start(plan, me, slots, blocks), window), :]
    query = dot(x, w_in[0]) * (HEAD_DIM ** (-0.5) * LOG2E)
    odd_lane = lax.broadcasted_iota(jnp.int32, (1, local), 1) // HEAD_DIM % 2 == 1
    q_even[...] = jnp.where(odd_lane, 0.0, query).astype(BF16)
    q_odd[...] = jnp.where(odd_lane, query, 0.0).astype(BF16)
    triple[0, :, 0:local] = query.astype(BF16)
    key = dot(x, w_in[1]).astype(BF16)
    triple[0, :, local : 2 * local] = key
    keys[0:window, :] = key
    value = dot(x, w_in[2]).astype(BF16)
    triple[0, :, 2 * local : 3 * local] = value
    values[0:window, :] = value
    left = lax.broadcasted_iota(jnp.int32, (1, LANES), 1) < HEAD_DIM
    lane_head = lax.broadcasted_iota(jnp.int32, (1, LANES), 1) // plan.group_lanes
    chunks = plan.key_chunks
    spans = list(zip(plan.cuts[:-1], plan.cuts[1:]))

    def scores_of(head):
        cols = slice(head // 2 * LANES, (head // 2 + 1) * LANES)
        q = (q_even, q_odd)[head % 2]
        pick = group_mask(plan, head)
        scores = []
        for k0, count, r0 in chunks:
            lhs = jnp.concatenate([q[r0:, cols], qhot[0, r0:window, :]], axis=1)
            rhs = jnp.concatenate(
                [keys[k0 : k0 + count, cols], kbias[0, k0 : k0 + count, :] * pick], axis=1
            )
            scores.append(dot(lhs, rhs, NT))
        return scores

    def soften(scores):
        tops, weights = [], [[] for _ in chunks]
        for i, (begin, end) in enumerate(spans):
            pieces = [scores[c][begin - chunks[c][2] : end - chunks[c][2]] for c in range(i + 1)]
            top = jnp.max(jnp.concatenate(pieces, axis=1), axis=-1, keepdims=True)
            tops.append(jnp.broadcast_to(top, (end - begin, LANES)))
            for c in range(i + 1):
                weights[c].append(jnp.exp2(pieces[c] - top).astype(BF16))
        return jnp.concatenate(tops, axis=0), [jnp.concatenate(w, axis=0) for w in weights]

    def mix(head, weights):
        cols = slice(head // 2 * LANES, (head // 2 + 1) * LANES)
        parts = []
        for (k0, count, _), weight in zip(chunks, weights):
            rhs = jnp.concatenate(
                [values[k0 : k0 + count, cols], jnp.ones((count, LANES), BF16)], axis=1
            )
            parts.append(dot(weight, rhs))
        rows = []
        for i, (begin, end) in enumerate(spans):
            pieces = [parts[c][begin - chunks[c][2] : end - chunks[c][2]] for c in range(i + 1)]
            rows.append(functools.reduce(jnp.add, pieces))
        return jnp.concatenate(rows, axis=0)

    state = {}

    def finish(head, top, mixed):
        total = mixed[:, LANES:]
        state[head] = mixed[:, :LANES] / total
        if head == 0:
            state["top"], state["total"] = top, total
        else:
            state["top"] = jnp.where(lane_head == head, top, state["top"])
            state["total"] = jnp.where(lane_head == head, total, state["total"])
        if head % 2 == 1:
            both = jnp.where(left, state[head - 1], state[head]) * valid[0].astype(F32)
            attention[0, :, (head // 2) * LANES : (head // 2 + 1) * LANES] = both.astype(BF16)

    heads = plan.heads
    scores = {h: scores_of(h) for h in range(min(2, heads))}
    soft, mixed = {}, {}
    for h in range(heads):
        soft[h] = soften(scores.pop(h))
        if h + 2 < heads:
            scores[h + 2] = scores_of(h + 2)
        mixed[h] = mix(h, soft[h][1])
        if h >= 1:
            finish(h - 1, soft[h - 1][0], mixed.pop(h - 1))
    finish(heads - 1, soft[heads - 1][0], mixed.pop(heads - 1))
    lse[0] = state["top"] + jnp.log2(state["total"])
    if last:
        put_windows(plan, me, slots, [before], whole[0], attention[0])

        @pl.when(pl.program_id(0) == len(slots) - 1)
        def _():
            scatter_blocks(plan, me, lambda rows: dot(whole[0][rows, :], w_out[...]), outs)


def per_slot(slots, shape):
    first = slots[0]
    return pl.BlockSpec((1,) + shape, lambda s: (s + first,) + (0,) * len(shape))


def attend(plan, layer, slots, me, blocks, input_weight, masks, away, output_weight=None, before=None):
    block = (plan.block, plan.width)
    n = len(slots)
    last = before is not None
    each = lambda shape: pl.BlockSpec((1,) + shape, lambda s: (s, 0, 0))
    shape = lambda *dims: result((n, plan.window) + dims, BF16, away)
    in_specs = [pl.BlockSpec(memory_space=SMEM)] + [full(block)] * len(blocks)
    in_specs += [layer_of(input_weight.shape[1:], layer)]
    in_specs += [per_slot(slots, m.shape[1:]) for m in masks]
    out_specs = [
        each((plan.window, 3 * plan.local)),
        each((plan.window, plan.local)),
        each((plan.window, LANES)),
    ]
    out_shape = [
        shape(3 * plan.local),
        shape(plan.local),
        result((n, plan.window, LANES), F32, away),
    ]
    scratch = [
        pltpu.VMEM((len(blocks) * plan.block, plan.width), BF16),
        pltpu.VMEM((plan.window, plan.local), BF16),
        pltpu.VMEM((plan.window, plan.local), BF16),
        pltpu.VMEM((plan.lanes, plan.local), BF16),
        pltpu.VMEM((plan.lanes, plan.local), BF16),
    ]
    args = [me, *blocks, input_weight, *masks]
    if last:
        in_specs += [layer_of(output_weight.shape[1:], layer), full(before.shape)]
        args += [output_weight, before]
        out_specs += [full(block)] * 4
        out_shape += [jax.ShapeDtypeStruct(block, BF16)] * 4
        scratch += [pltpu.VMEM((plan.total, plan.local), BF16)]
    area = plan.window * plan.lanes * plan.heads
    return pl.pallas_call(
        functools.partial(attend_kernel, plan, slots, len(blocks)),
        grid=(n,),
        in_specs=in_specs,
        out_specs=out_specs,
        out_shape=out_shape,
        scratch_shapes=scratch,
        compiler_params=params(20),
        cost_estimate=cost(3 * n),
        name="attend",
    )(*args)


def three_parts(value):
    high = value.astype(BF16)
    rest = value - high.astype(F32)
    middle = rest.astype(BF16)
    low = (rest - middle.astype(F32)).astype(BF16)
    return high.astype(F32), middle.astype(F32), low.astype(F32)


def attend_back_kernel(plan, slots, blocks, *refs):
    me, refs = refs[0], refs[1:]
    placed, refs = refs[:blocks], refs[blocks:]
    w_out, qhot, kbias, valid, triple, attention, lse = refs[:7]
    refs = refs[7:]
    last = slots[-1] == plan.seqs - 1
    if last:
        w_in, before, refs = refs[0], refs[1 : 1 + slots[0]], refs[1 + slots[0] :]
    triple_grad, refs = refs[0], refs[1:]
    if last:
        outs, refs = refs[:4], refs[4:]
    gathered, queries, grads, query_side, grad_side, key_turned, *whole = refs
    window, local, lanes = plan.window, plan.local, plan.lanes

    @pl.when(pl.program_id(0) == 0)
    def _():
        place_blocks(plan, me, placed, gathered)
        queries[window:, :] = jnp.zeros((lanes - window, local), BF16)
        grads[window:, :] = jnp.zeros((lanes - window, local), BF16)
        query_side[window:, :] = jnp.zeros((lanes - window, LANES), BF16)
        grad_side[window:, :] = jnp.zeros((lanes - window, LANES), BF16)

    mask = valid[0].astype(F32)
    head_grad = dot(gathered[pl.ds(window_start(plan, me, slots, blocks), window), :], w_out[...], NT)
    head_grad = head_grad * jnp.concatenate([mask] * (local // LANES), axis=1)
    head_grad = head_grad.astype(BF16)
    grads[0:window, :] = head_grad
    queries[0:window, :] = triple[0, :, 0:local]
    key_turned[...] = triple[0, :, local : 2 * local].T
    product = head_grad.astype(F32) * attention[0].astype(F32)
    high = product.astype(BF16)
    low = (product - high.astype(F32)).astype(BF16)
    spread = jnp.where(
        lax.broadcasted_iota(jnp.int32, (local, LANES), 0) // HEAD_DIM
        == lax.broadcasted_iota(jnp.int32, (local, LANES), 1) // plan.group_lanes,
        1.0,
        0.0,
    ).astype(BF16)
    inner = dot(high, spread) + dot(low, spread)
    slot = lax.broadcasted_iota(jnp.int32, (1, LANES), 1) % plan.group_lanes
    a, b, c = three_parts(-inner)
    grad_side[0:window, :] = jnp.where(
        slot == 0, a, jnp.where(slot == 1, b, jnp.where(slot == 2, c, 0.0))
    ).astype(BF16)
    a, b, c = three_parts(-lse[0])
    n = plan.frames
    query_side[0:window, :] = jnp.where(
        slot < n,
        qhot[0, 0:window, :].astype(F32),
        jnp.where(slot == n, a, jnp.where(slot == n + 1, b, jnp.where(slot == n + 2, c, 0.0))),
    ).astype(BF16)
    left = lax.broadcasted_iota(jnp.int32, (1, LANES), 1) < HEAD_DIM
    sides = [jnp.where(left, 1.0, 0.0).astype(BF16), jnp.where(left, 0.0, 1.0).astype(BF16)]
    chunks = plan.query_chunks
    ends = [0] + [c[2] for c in chunks]

    def products(head):
        half = head % 2
        tile = head // 2 * LANES
        cols = slice(tile, tile + LANES)
        pick = group_mask(plan, head)
        ones = jnp.where(slot < 3, pick.astype(F32), 0.0).astype(BF16)
        key_side = jnp.concatenate(
            [
                triple[0, :, local + tile : local + tile + LANES] * sides[half],
                kbias[0, 0:window, :] * pick,
            ],
            axis=1,
        )
        value_side = jnp.concatenate(
            [
                triple[0, :, 2 * local + tile : 2 * local + tile + LANES] * sides[half],
                jnp.broadcast_to(ones, (window, LANES)),
            ],
            axis=1,
        )
        scores, prob_grads = [], []
        for q0, count, reach in chunks:
            rows = slice(q0, q0 + count)
            rhs = jnp.concatenate([queries[rows, cols], query_side[rows, :]], axis=1)
            scores.append(dot(key_side[:reach], rhs, NT))
        for q0, count, reach in chunks:
            rows = slice(q0, q0 + count)
            rhs = jnp.concatenate([grads[rows, cols], grad_side[rows, :]], axis=1)
            prob_grads.append(dot(value_side[:reach], rhs, NT))
        return scores, prob_grads

    def pointwise(scores, prob_grads):
        probs = [jnp.exp2(s) for s in scores]
        score_grads = [(p * g).astype(BF16) for p, g in zip(probs, prob_grads)]
        return [p.astype(BF16) for p in probs], score_grads

    def add_rows(parts):
        rows = []
        for i in range(len(chunks)):
            pieces = [p[ends[i] : ends[i + 1]] for p in parts[i:]]
            rows.append(functools.reduce(jnp.add, pieces))
        return jnp.concatenate(rows, axis=0)

    def gradients(head, probs, score_grads):
        tile = head // 2 * LANES
        cols = slice(tile, tile + LANES)
        value_parts, key_parts, query_parts = [], [], []
        turned = key_turned[tile + head % 2 * HEAD_DIM : tile + (head % 2 + 1) * HEAD_DIM, :]
        for (q0, count, reach), prob in zip(chunks, probs):
            value_parts.append(dot(prob, grads[q0 : q0 + count, cols]))
        for (q0, count, reach), score_grad in zip(chunks, score_grads):
            key_parts.append(dot(score_grad, queries[q0 : q0 + count, cols]))
        for (q0, count, reach), score_grad in zip(chunks, score_grads):
            query_parts.append(dot(turned[:, :reach], score_grad))
        return jnp.concatenate(query_parts, axis=1), add_rows(key_parts), add_rows(value_parts)

    heads = plan.heads
    found = [products(h) for h in range(heads)]
    pointed = [pointwise(*f) for f in found]
    for tile in range(heads // 2):
        even, odd = (gradients(h, *pointed[h]) for h in (2 * tile, 2 * tile + 1))
        query = jnp.concatenate([even[0], odd[0]], axis=0).T[:window] * HEAD_DIM ** (-0.5)
        key = jnp.where(left, even[1], odd[1]) * LN2
        value = jnp.where(left, even[2], odd[2])
        for t, grad in enumerate((query, key, value)):
            at = t * local + tile * LANES
            triple_grad[0, :, at : at + LANES] = grad.astype(BF16)
    if last:
        put_windows(plan, me, slots, before, whole[0], triple_grad[0])

        @pl.when(pl.program_id(0) == len(slots) - 1)
        def _():
            def back(rows):
                total = dot(whole[0][rows, 0:local], w_in[0], NT)
                for t in (1, 2):
                    total = total + dot(whole[0][rows, t * local : (t + 1) * local], w_in[t], NT)
                return total

            scatter_blocks(plan, me, back, outs)


def attend_back(plan, layer, slots, me, blocks, output_weight, masks, saved, away, input_weight=None, before=None):
    block = (plan.block, plan.width)
    n = len(slots)
    last = before is not None
    each = lambda shape: pl.BlockSpec((1,) + shape, lambda s: (s, 0, 0))
    in_specs = [pl.BlockSpec(memory_space=SMEM)] + [full(block)] * len(blocks)
    in_specs += [layer_of(output_weight.shape[1:], layer)]
    in_specs += [per_slot(slots, m.shape[1:]) for m in masks]
    in_specs += [per_slot([max(slots[0] - 1, 0)], a.shape[1:]) for a in saved]
    out_specs = [each((plan.window, 3 * plan.local))]
    out_shape = [jax.ShapeDtypeStruct((n, plan.window, 3 * plan.local), BF16)]
    scratch = [
        pltpu.VMEM((len(blocks) * plan.block, plan.width), BF16),
        pltpu.VMEM((plan.lanes, plan.local), BF16),
        pltpu.VMEM((plan.lanes, plan.local), BF16),
        pltpu.VMEM((plan.lanes, LANES), BF16),
        pltpu.VMEM((plan.lanes, LANES), BF16),
        pltpu.VMEM((plan.local, plan.window), BF16),
    ]
    args = [me, *blocks, *far([output_weight, *masks, *saved])]
    if last:
        in_specs += [layer_of(input_weight.shape[1:], layer)] + [full(w.shape) for w in before]
        args += [*far([input_weight]), *before]
        out_specs += [full(block)] * 4
        out_shape += [jax.ShapeDtypeStruct(block, BF16)] * 4
        scratch += [pltpu.VMEM((plan.total, 3 * plan.local), BF16)]
    area = plan.window * plan.lanes * plan.heads
    return pl.pallas_call(
        functools.partial(attend_back_kernel, plan, slots, len(blocks)),
        grid=(n,),
        in_specs=in_specs,
        out_specs=out_specs,
        out_shape=out_shape,
        scratch_shapes=scratch,
        compiler_params=params(28),
        cost_estimate=cost(6 * n),
        name="attend_back",
    )(*args)


FF_STEPS = 4


def forward_kernel(plan, last, stream, part_a, part_b, part_c, out_bias, gain, shift, up, up_bias, down, down_bias, next_gain, next_shift, middle, lifted, hidden, slope, *rest):
    outs, total = rest[:-1], rest[-1]
    step = pl.program_id(0)

    @pl.when(step == 0)
    def _():
        projected = part_a[...].astype(F32) + part_b[...].astype(F32) + part_c[...].astype(F32)
        values = stream[...] + (projected + out_bias[...])
        middle[...] = values
        center, scale = norm_stats(values)
        lifted[...] = (center * scale * gain[1:2, :] + shift[1:2, :]).astype(BF16)
        total[...] = values + down_bias[...]

    before = dot(lifted[...], up[...]) + up_bias[...]
    cdf = 0.5 + 0.5 * lax.erf(before * (2.0**-0.5))
    density = jnp.exp2(before * before * (-0.5 * LOG2E)) * (2.0 * math.pi) ** -0.5
    act = (before * cdf).astype(BF16)
    hidden[...] = act
    slope[...] = (cdf + before * density).astype(BF16)
    total[...] += dot(act, down[...])

    @pl.when(step == FF_STEPS - 1)
    def _():
        values = total[...]
        if last:
            outs[0][...] = values.astype(BF16)[: plan.rows]
        else:
            outs[0][...] = values
            center, scale = norm_stats(values)
            outs[1][...] = (center * scale * next_gain[0:1, :] + next_shift[0:1, :]).astype(BF16)


def forward_rest(plan, layer, layers, stream, parts, output_bias, gain, shift, up, up_bias, down, down_bias):
    last = layer == layers - 1
    block = (plan.block, plan.width)
    cols = plan.hidden // FF_STEPS
    follow = min(layer + 1, layers - 1)
    wide = pl.BlockSpec((plan.block, cols), lambda j: (0, j))
    row = lambda width: layer_of((1, width), layer)
    if last:
        tail_specs = [full((plan.rows, plan.width))]
        tail = [jax.ShapeDtypeStruct((plan.rows, plan.width), BF16)]
    else:
        tail_specs = [full(block), full(block)]
        tail = [jax.ShapeDtypeStruct(block, F32), jax.ShapeDtypeStruct(block, BF16)]
    return pl.pallas_call(
        functools.partial(forward_kernel, plan, last),
        grid=(FF_STEPS,),
        in_specs=[full(block)] * 4
        + [
            row(plan.width),
            layer_of(gain.shape[1:], layer),
            layer_of(gain.shape[1:], layer),
            pl.BlockSpec((None, plan.width, cols), lambda j: (layer, 0, j)),
            pl.BlockSpec((None, 1, cols), lambda j: (layer, 0, j)),
            pl.BlockSpec((None, cols, plan.width), lambda j: (layer, j, 0)),
            row(plan.width),
            layer_of(gain.shape[1:], follow),
            layer_of(gain.shape[1:], follow),
        ],
        out_specs=[full(block), full(block), wide, wide] + tail_specs,
        out_shape=[
            result(block, F32),
            result(block, BF16),
            result((plan.block, plan.hidden), BF16),
            result((plan.block, plan.hidden), BF16),
        ]
        + tail,
        scratch_shapes=[pltpu.VMEM(block, F32)],
        compiler_params=params(20),
        cost_estimate=cost(5),
        name="forward_rest",
    )(stream, *parts, *far([output_bias, gain, shift]), up, *far([up_bias]), down, *far([down_bias, gain, shift]))


def back_kernel(plan, carry, middle, slope, gain, up, down, low, before_low, middle_grad, middle_low, sums, up_bias, total):
    step = pl.program_id(0)

    @pl.when(step == 0)
    def _():
        low[...] = carry[...].astype(BF16)
        total[...] = jnp.zeros(total.shape, F32)

    before_grad = dot(low[...], down[...], NT) * slope[...].astype(F32)
    up_bias[...] = jnp.sum(before_grad, axis=0, keepdims=True)
    narrow = before_grad.astype(BF16)
    before_low[...] = narrow
    total[...] += dot(narrow, up[...], NT)

    @pl.when(step == FF_STEPS - 1)
    def _():
        center, scale = norm_stats(middle[...])
        grad, gain_sum, shift_sum = norm_back(total[...], center, scale, gain[1:2, :])
        carried = carry[...]
        grad = carried + grad
        middle_grad[...] = grad
        middle_low[...] = grad.astype(BF16)
        sums[...] = jnp.zeros(sums.shape, F32)
        sums[0:1, :] = gain_sum
        sums[1:2, :] = shift_sum
        sums[2:3, :] = jnp.sum(grad, axis=0, keepdims=True)
        sums[3:4, :] = jnp.sum(carried, axis=0, keepdims=True)


def back_rest(plan, layer, carry, middle, slope, gain, up, down, away):
    block = (plan.block, plan.width)
    cols = plan.hidden // FF_STEPS
    wide = pl.BlockSpec((plan.block, cols), lambda j: (0, j))
    return pl.pallas_call(
        functools.partial(back_kernel, plan),
        grid=(FF_STEPS,),
        in_specs=[
            full(block),
            full(block),
            wide,
            layer_of(gain.shape[1:], layer),
            pl.BlockSpec((None, plan.width, cols), lambda j: (layer, 0, j)),
            pl.BlockSpec((None, cols, plan.width), lambda j: (layer, j, 0)),
        ],
        out_specs=[
            full(block),
            wide,
            full(block),
            full(block),
            full((8, plan.width)),
            pl.BlockSpec((1, cols), lambda j: (0, j)),
        ],
        out_shape=[
            jax.ShapeDtypeStruct(block, BF16),
            jax.ShapeDtypeStruct((plan.block, plan.hidden), BF16),
            jax.ShapeDtypeStruct(block, F32),
            jax.ShapeDtypeStruct(block, BF16),
            jax.ShapeDtypeStruct((8, plan.width), F32),
            jax.ShapeDtypeStruct((1, plan.hidden), F32),
        ],
        scratch_shapes=[pltpu.VMEM(block, F32)],
        compiler_params=params(20),
        cost_estimate=cost(6),
        name="back_rest",
    )(carry, *far((middle, slope), away), *far((gain, up, down)))


SMALL_ROWS = 8
CUT = 3


def carry_kernel(plan, wide, me, env_id, part_a, part_b, part_c, stream, middle_grad, gain, *rest):
    others, outs = rest[: len(rest) - 2], rest[-2:]
    carry, sums = outs
    upstream = part_a[...].astype(F32) + part_b[...].astype(F32) + part_c[...].astype(F32)
    center, scale = norm_stats(stream[...])
    grad, gain_sum, shift_sum = norm_back(upstream, center, scale, gain[0:1, :])
    grad = middle_grad[...] + grad
    carry[...] = grad[: carry.shape[0]]
    sums[...] = jnp.zeros(sums.shape, F32)
    sums[0:1, :] = gain_sum
    sums[1:2, :] = shift_sum
    if not others:
        return
    row = lax.broadcasted_iota(jnp.int32, (plan.block, plan.width), 0)
    place = me[0] * plan.rows + row
    envs = sums.shape[0] - SMALL_ROWS * (1 + len(others))
    line = lax.broadcasted_iota(jnp.int32, (envs, plan.width), 0)
    total = jnp.zeros((envs, plan.width), F32)
    for s in range(plan.seqs):
        inside = (row < plan.rows) & (place >= s * plan.length)
        inside = inside & (place < (s + 1) * plan.length)
        part = jnp.sum(jnp.where(inside, grad, 0.0), axis=0, keepdims=True)
        total = total + jnp.where(line == env_id[0:1, s : s + 1], part, 0.0)
    at = SMALL_ROWS
    for ref in others:
        if ref.shape[0] == 1:
            for i in range(SMALL_ROWS):
                sums[at + i : at + i + 1, 0:wide] = ref[:, i * wide : (i + 1) * wide]
        else:
            sums[at : at + SMALL_ROWS, :] = ref[...]
        at += SMALL_ROWS
    sums[at : at + envs, :] = total


def carry_back(plan, layer, me, env_id, envs, parts, stream, middle_grad, gain, others, away):
    block = (plan.block, plan.width)
    first = layer == 0
    rows = plan.rows if first else plan.block
    wide = plan.hidden // SMALL_ROWS
    assert wide <= plan.width and wide % LANES == 0
    small = SMALL_ROWS * (1 + len(others)) + (envs if first else 0)
    return pl.pallas_call(
        functools.partial(carry_kernel, plan, wide),
        grid=(1,),
        in_specs=[pl.BlockSpec(memory_space=SMEM), full(env_id.shape)]
        + [full(block)] * 5
        + [layer_of(gain.shape[1:], layer)]
        + [full(o.shape) for o in others],
        out_specs=[full((rows, plan.width)), full((small, plan.width))],
        out_shape=[
            jax.ShapeDtypeStruct((rows, plan.width), F32),
            jax.ShapeDtypeStruct((small, plan.width), F32),
        ],
        compiler_params=params(16),
        cost_estimate=cost(2),
        name="carry_back",
    )(me, *far([env_id]), *parts, *far([stream], away), middle_grad, *far([gain, *others]))


def emit_small_kernel(plan, layers, envs, small, env, gain, shift, out_bias, up_bias, down_bias):
    wide = plan.hidden // SMALL_ROWS
    at = SMALL_ROWS
    for layer in range(layers):
        second = at
        up = at + SMALL_ROWS
        first = 0 if layer == 0 else at + 2 * SMALL_ROWS
        at += (2 if layer == 0 else 3) * SMALL_ROWS
        gain[layer, 0:1, :] = small[first : first + 1, :]
        shift[layer, 0:1, :] = small[first + 1 : first + 2, :]
        gain[layer, 1:2, :] = small[second : second + 1, :]
        shift[layer, 1:2, :] = small[second + 1 : second + 2, :]
        out_bias[layer : layer + 1, :] = small[second + 2 : second + 3, :]
        down_bias[layer : layer + 1, :] = small[second + 3 : second + 4, :]
        for i in range(SMALL_ROWS):
            up_bias[layer : layer + 1, i * wide : (i + 1) * wide] = small[up + i : up + i + 1, 0:wide]
    env[...] = small[at : at + envs, :]


def emit_small(plan, layers, envs, small):
    shapes = [
        (envs, plan.width),
        (layers, 2, plan.width),
        (layers, 2, plan.width),
        (layers, plan.width),
        (layers, plan.hidden),
        (layers, plan.width),
    ]
    return pl.pallas_call(
        functools.partial(emit_small_kernel, plan, layers, envs),
        grid=(1,),
        in_specs=[full(small.shape)],
        out_specs=[full(s) for s in shapes],
        out_shape=[jax.ShapeDtypeStruct(s, F32) for s in shapes],
        compiler_params=params(8),
        cost_estimate=cost(1),
        name="emit_small",
    )(small)


def feed_grads_kernel(plan, me, lifted, before_low, low, hidden, keep, send, lifted_t, low_t):
    @pl.when(pl.program_id(0) == 0)
    def _():
        lifted_t[...] = lifted[...].T
        low_t[...] = low[...].T

    up = dot(lifted_t[...], before_low[...]).astype(BF16)
    down = dot(low_t[...], hidden[...]).astype(BF16)

    @pl.when(me[0] % 2 == 0)
    def _():
        keep[...] = up
        send[...] = down

    @pl.when(me[0] % 2 == 1)
    def _():
        keep[...] = down
        send[...] = up


def feed_grads(plan, me, lifted, before_low, low, hidden, away):
    block = (plan.block, plan.width)
    cols = plan.hidden // FF_STEPS
    wide = pl.BlockSpec((plan.block, cols), lambda j: (0, j))
    out = pl.BlockSpec((plan.width, cols), lambda j: (0, j))
    shape = result((plan.width, plan.hidden), BF16, True)
    return pl.pallas_call(
        functools.partial(feed_grads_kernel, plan),
        grid=(FF_STEPS,),
        in_specs=[pl.BlockSpec(memory_space=SMEM), full(block), wide, full(block), wide],
        out_specs=[out, out],
        out_shape=[shape, shape],
        scratch_shapes=[pltpu.VMEM((plan.width, plan.block), BF16)] * 2,
        compiler_params=params(16),
        cost_estimate=cost(5),
        name="feed_grads",
    )(me, *far([lifted], away), before_low, low, *far([hidden], away))


def head_grads_kernel(plan, kinds, beside, digit, *refs):
    me, refs = refs[0], refs[1:]
    scratch, refs = refs[-1], refs[:-1]
    columns = []
    for count in kinds:
        blocks, windows, refs = refs[:4], refs[4 : 4 + count], refs[4 + count :]
        place_blocks(plan, me, blocks, scratch)
        rights = [ref[i] for ref in windows for i in range(ref.shape[0])]
        total = None
        for slot, right in enumerate(rights):
            start = pl.multiple_of(plan.sequence(slot, me[0] // 2) * plan.stride, 16)
            part = dot(scratch[pl.ds(start, plan.window), :].T, right)
            total = part if total is None else total + part
        columns.append(total.astype(BF16))
    if beside:
        columns.append(refs[0][...])
        refs = refs[1:]
    value = jnp.concatenate(columns, axis=1) if len(columns) > 1 else columns[0]
    n = len(refs)
    if n == 1:
        refs[0][...] = value
        return
    count = plan.width // n
    for mine in range(n):

        @pl.when(digit[0] == mine)
        def _(mine=mine):
            for j, ref in enumerate(refs):
                at = (mine ^ j) * count
                ref[...] = value[at : at + count]


def head_grads(plan, me, digit, pieces, pairs, beside=()):
    cols = sum(p[1][0].shape[2] for p in pairs) + sum(b.shape[1] for b in beside)
    shape = (plan.width // pieces, cols)
    flat = [a for p in pairs for a in (*p[0], *p[1])] + list(beside)
    return pl.pallas_call(
        functools.partial(head_grads_kernel, plan, [len(p[1]) for p in pairs], len(beside)),
        grid=(1,),
        in_specs=[pl.BlockSpec(memory_space=SMEM)] * 2 + [full(a.shape) for a in flat],
        out_specs=[full(shape)] * pieces,
        out_shape=[jax.ShapeDtypeStruct(shape, BF16)] * pieces,
        scratch_shapes=[pltpu.VMEM((plan.total, plan.width), BF16)],
        compiler_params=params(20),
        cost_estimate=cost(5),
        name="head_grads",
    )(digit, me, *far(flat))


def swap(value, bit):
    size = lax.axis_size("head")
    return lax.ppermute(value, "head", [(i, i ^ bit) for i in range(size)])


def scatter(outs):
    to_diagonal, to_core, to_across, mine = outs
    first = swap(to_diagonal, 1)
    second = swap(to_core, 1)
    pair = (to_across.astype(F32) + first.astype(F32)).astype(BF16)
    return mine, second, swap(pair, 2)


def tie(*trees):
    return lax.optimization_barrier(trees)


class Bits:
    def __init__(self):
        self.heads = lax.axis_size("head")
        self.size = lax.axis_size("seq") * self.heads
        self.place = lax.axis_index("seq") * self.heads + lax.axis_index("head")
        self.place = self.place.astype(jnp.int32)
        seq = [self.heads << i for i in range((self.size // self.heads).bit_length() - 1)]
        self.core, self.across = (1, 1), (2, 2)
        self.seq = [(seq[0], seq[1]), (seq[1], seq[0])] + [(m, m) for m in seq[2:]]

    def bit(self, mask):
        return jnp.where((self.place & mask) > 0, 1, 0).astype(jnp.int32).reshape(1)

    def digit(self, step):
        core = self.place & 1
        value = jnp.int32(0)
        for i, (zero, one) in enumerate(step):
            mask = jnp.where(core == 0, zero, one)
            value = value + jnp.where((self.place & mask) > 0, 1 << i, 0)
        return value.astype(jnp.int32).reshape(1)

    def send(self, value, step, j):
        def partner(place):
            for i, masks in enumerate(step):
                if j >> i & 1:
                    place ^= masks[place & 1]
            return place

        pairs = [(p, partner(p)) for p in range(self.size)]
        return lax.ppermute(value, ("seq", "head"), pairs)


def cut(shape, pieces):
    if shape[0] % (16 * pieces) == 0:
        return 0
    if shape[1] % (LANES * pieces) == 0:
        return 1
    return None


def piece_at(shape, pieces, index):
    dim = cut(shape, pieces) if pieces > 1 else 0
    count = shape[dim] // pieces
    part = tuple(count if d == dim else shape[d] for d in range(2))
    if pieces == 1:
        return (slice(None), slice(None)), part
    window = pl.ds(pl.multiple_of(index * count, 16 if dim == 0 else LANES), count)
    return tuple(window if d == dim else slice(None) for d in range(2)), part


def fold_kernel(pieces, dim, digit, *refs):
    ins, outs = refs[: len(refs) - pieces], refs[len(refs) - pieces :]
    count = ins[0].shape[dim] // pieces
    for j, out in enumerate(outs):
        place = digit[0] ^ j if pieces > 1 else 0
        at = pl.ds(pl.multiple_of(place * count, LANES if dim else 16), count)
        where = (slice(None), at) if dim else (at, slice(None))
        total = ins[0][where].astype(F32)
        for ref in ins[1:]:
            total = total + ref[where].astype(F32)
        out[...] = total.astype(BF16)


def large(shape):
    return shape[0] * shape[1] >= 192 * 1024


def in_columns(shape, dim):
    return shape[1] // 512 if dim == 0 and large(shape) and shape[1] % 512 == 0 else 1


def fold(digit, pieces, arrays):
    rows, cols = arrays[0].shape
    dim = cut((rows, cols), pieces)
    part = (rows, cols // pieces) if dim else (rows // pieces, cols)
    steps = in_columns((rows, cols), dim)
    of = lambda shape: pl.BlockSpec((shape[0], shape[1] // steps), lambda j: (0, j))
    return pl.pallas_call(
        functools.partial(fold_kernel, pieces, dim),
        grid=(steps,),
        in_specs=[pl.BlockSpec(memory_space=SMEM)] + [of((rows, cols))] * len(arrays),
        out_specs=[of(part)] * pieces,
        out_shape=[result(part, BF16, large(part))] * pieces,
        compiler_params=params(16),
        cost_estimate=cost(2 if large(arrays[0].shape) else 1),
        name="fold",
    )(digit, *far(arrays, large((rows, cols))))


def join_kernel(dim, digit, own, came, out):
    count = own.shape[dim]
    for j, ref in enumerate((own, came)):
        at = pl.ds(pl.multiple_of((digit[0] ^ j) * count, LANES if dim else 16), count)
        out[(slice(None), at) if dim else (at, slice(None))] = ref[...]


def join(digit, dim, own, came):
    rows, cols = own.shape
    whole = (rows, 2 * cols) if dim else (2 * rows, cols)
    steps = in_columns(whole, dim)
    of = lambda shape: pl.BlockSpec((shape[0], shape[1] // steps), lambda j: (0, j))
    return pl.pallas_call(
        functools.partial(join_kernel, dim),
        grid=(steps,),
        in_specs=[pl.BlockSpec(memory_space=SMEM), of((rows, cols)), of((rows, cols))],
        out_specs=of(whole),
        out_shape=result(whole, BF16, large(whole)),
        compiler_params=params(16),
        cost_estimate=cost(2 if large(whole) else 1),
        name="join",
    )(digit, *far((own, came), large((rows, cols))))


class Chain:
    def __init__(self, bits, plan, keep, send):
        self.bits, self.plan = bits, plan
        self.state = [keep, send]
        self.dims = [None]
        self.at = -1
        self.back = False
        self.done = False

    def work(self):
        bits, plan = self.bits, self.plan
        if not self.back:
            self.at += 1
            if self.at == 0:
                return
            if self.at == len(plan):
                self.at -= 1
                self.back = True
                (own,) = fold(bits.digit([plan[-1]]), 1, self.state)
                self.state = [own, own]
                return
            self.dims.append(cut(self.state[0].shape, 2))
            self.state = list(fold(bits.digit([plan[self.at]]), 2, self.state))
            return
        if self.at == 0:
            self.done = True
            return
        own = join(bits.digit([plan[self.at]]), self.dims[self.at], *self.state)
        self.at -= 1
        self.state = [own, own]

    def exchange(self):
        if not self.done:
            came = self.bits.send(self.state[1], [self.plan[self.at]], 1)
            self.state = [self.state[0], came]


def small_steps(bits):
    return [[b] for b in [bits.core, bits.across] + bits.seq]


def sum_small(bits, step, value):
    came = [bits.send(value, step, j) for j in range(1, 1 << len(step))]
    return functools.reduce(jnp.add, came, value)


def emit_feed_kernel(plan, count, me, digits, *refs):
    sources, (up, down, turned) = refs[: 2 * count], refs[-3:]
    size = plan.width // count
    own, other = sources[:count], sources[count:]
    for core, (ups, downs) in enumerate(((own, other), (other, own))):

        @pl.when(me[0] % 2 == core)
        def _(ups=ups, downs=downs):
            for j in range(count):
                rows = pl.ds(pl.multiple_of((digits[0] ^ j) * size, 16), size)
                up[rows, :] = ups[j][...].astype(F32)
                rows = pl.ds(pl.multiple_of((digits[1] ^ j) * size, 16), size)
                turned[rows, :] = downs[j][...]

    eye = jnp.where(
        lax.broadcasted_iota(jnp.int32, (plan.width, plan.width), 0)
        == lax.broadcasted_iota(jnp.int32, (plan.width, plan.width), 1),
        1.0,
        0.0,
    ).astype(BF16)
    down[...] = dot(turned[...], eye, TN)


def emit_feed(plan, me, digits, layer, layers, sources, before):
    cols = plan.hidden // FF_STEPS
    of = lambda a: pl.BlockSpec((a.shape[0], cols), lambda j: (0, j))
    anywhere = pl.BlockSpec(memory_space=pl.ANY)
    smem = pl.BlockSpec(memory_space=SMEM)

    def kernel(me_ref, digits_ref, *refs):
        ins, outs = refs[: len(sources)], refs[len(sources) + len(before) :]
        emit_feed_kernel(plan, len(sources) // 2, me_ref, digits_ref, *ins, *outs)

    return pl.pallas_call(
        kernel,
        grid=(FF_STEPS,),
        in_specs=[smem, smem] + [of(a) for a in sources] + [anywhere] * len(before),
        out_specs=[
            pl.BlockSpec((None, plan.width, cols), lambda j: (layer, 0, j)),
            pl.BlockSpec((None, cols, plan.width), lambda j: (layer, j, 0)),
        ],
        out_shape=[
            jax.ShapeDtypeStruct((layers, plan.width, plan.hidden), F32),
            jax.ShapeDtypeStruct((layers, plan.hidden, plan.width), F32),
        ],
        scratch_shapes=[pltpu.VMEM((plan.width, cols), BF16)],
        input_output_aliases={2 + len(sources) + i: i for i in range(len(before))},
        compiler_params=params(16),
        cost_estimate=cost(4),
        name="emit_feed",
    )(me, digits, *far(sources), *before)


def emit_heads_kernel(plan, layers, digit, *refs):
    sources, (into, out) = refs[:-2], refs[-2:]
    local = plan.local
    count = plan.width // len(sources)

    def put(ref, rows):
        for layer in range(layers):
            at = layer * 4 * local
            for t in range(3):
                into[layer, t, rows, :] = ref[:, at + t * local : at + (t + 1) * local].astype(F32)
            out[layer, :, rows] = ref[:, at + 3 * local : at + 4 * local].astype(F32).T

    if len(sources) == 1:
        put(sources[0], slice(0, count))
        return
    for mine in range(2):

        @pl.when(digit[0] == mine)
        def _(mine=mine):
            for j, ref in enumerate(sources):
                put(ref, slice((mine ^ j) * count, ((mine ^ j) + 1) * count))


def emit_heads(plan, digit, layers, sources):
    shapes = [(layers, 3, plan.width, plan.local), (layers, plan.local, plan.width)]
    return pl.pallas_call(
        functools.partial(emit_heads_kernel, plan, layers),
        grid=(1,),
        in_specs=[pl.BlockSpec(memory_space=SMEM)] + [full(a.shape) for a in sources],
        out_specs=[full(s) for s in shapes],
        out_shape=[jax.ShapeDtypeStruct(s, F32) for s in shapes],
        compiler_params=params(24),
        cost_estimate=cost(2),
        name="emit_heads",
    )(digit, *far(sources))


def body(
    tokens,
    actions,
    action_mask,
    frame_mask,
    environment_id,
    environment_embed,
    norm_gain,
    norm_bias,
    input_weight,
    output_weight,
    output_bias,
    up_weight,
    up_bias,
    down_weight,
    down_bias,
    cotangent,
):
    rows, width = tokens.shape
    seqs, frames, _ = actions.shape
    layers = input_weight.shape[0]
    envs = environment_embed.shape[0]
    plan = Plan(
        rows,
        lax.axis_size("head"),
        seqs,
        frames,
        width,
        input_weight.shape[3],
        up_weight.shape[2],
    )
    bits = Bits()
    me = lax.axis_index("head").astype(jnp.int32).reshape(1)
    as_rows = lambda t: t.reshape(layers, 1, -1)
    env_row = environment_id.reshape(1, seqs)
    stream, normed, *masks = prologue(
        plan,
        me,
        action_mask,
        frame_mask,
        env_row,
        tokens,
        actions,
        environment_embed,
        norm_gain,
        norm_bias,
    )
    own_slot, other_slots = [0], [1, 2]
    saved = []
    for layer in range(layers):
        away = False
        core, across = swap(normed, 1), swap(normed, 2)
        first = attend(plan, layer, own_slot, me, (normed, core), input_weight, masks, away)
        across, first = tie(across, first)
        blocks = (normed, core, across, swap(across, 1))
        *second, to_diagonal, to_core, to_across, mine = attend(
            plan,
            layer,
            other_slots,
            me,
            blocks,
            input_weight,
            masks,
            away,
            output_weight,
            first[1],
        )
        parts = scatter((to_diagonal, to_core, to_across, mine))
        middle, lifted, hidden, slope, *tail = forward_rest(
            plan,
            layer,
            layers,
            stream,
            parts,
            as_rows(output_bias),
            norm_gain,
            norm_bias,
            up_weight,
            as_rows(up_bias),
            down_weight,
            as_rows(down_bias),
        )
        saved.append((stream, blocks, first, second, middle, lifted, hidden, slope))
        if layer < layers - 1:
            stream, normed = tail
    mixed = tail[0]
    carry = jnp.pad(cotangent.astype(F32), ((0, plan.block - rows), (0, 0)))
    by_steps = len(bits.seq) == 3
    zero = jnp.zeros_like(me)
    stream, blocks, first, second, middle, lifted, hidden, slope = saved[-1]
    last = layers - 1

    def feed_back(layer, carry):
        stream, blocks, first, second, middle, lifted, hidden, slope = saved[layer]
        away = layer < last
        low, before_low, middle_grad, middle_low, second_sums, up_sums = back_rest(
            plan, layer, carry, middle, slope, norm_gain, up_weight, down_weight, away
        )
        core, across = swap(middle_low, 1), swap(middle_low, 2)
        lifted, core = tie(lifted, core)
        by_chain = by_steps and layer == 0
        feed = feed_grads(
            plan, me if by_chain else zero, lifted, before_low, low, hidden, away
        )
        core, feed = tie(core, feed)
        return middle_grad, middle_low, core, across, feed, second_sums, up_sums

    def own_back(layer, middle_low, core):
        return attend_back(
            plan,
            layer,
            [0],
            me,
            (middle_low, core),
            output_weight,
            masks,
            saved[layer][2],
            True,
        )[0]

    def start(chain, value):
        chain.state, value = tie(chain.state, value)
        chain.work()
        chain.state, value = tie(chain.state, value)
        chain.exchange()
        return value

    feed_plan = [bits.core] + bits.seq[:2] + [bits.across] + bits.seq[2:]
    held = {}

    def finish(state):
        middle_grad, middle_low, core, across, own_grad, last_sums = state
        heads, sums = {}, {}
        feed = None
        for layer in reversed(range(layers)):
            stream, blocks, first, second, middle, lifted, hidden, slope = saved[layer]
            tail = by_steps and layer == 0
            if layer < last:
                middle_grad, middle_low, core, across, feed, *last_sums = feed_back(layer, carry)
                if tail:
                    feed = Chain(bits, feed_plan, *feed)
                    core = start(feed, core)
                own_grad = own_back(layer, middle_low, core)
            across, own_grad = tie(across, own_grad)
            middle_blocks = (middle_low, core, across, swap(across, 1))
            if tail:
                middle_blocks = start(feed, middle_blocks)
            both_grad, *outs = attend_back(
                plan,
                layer,
                [1, 2],
                me,
                middle_blocks,
                output_weight,
                masks,
                second,
                True,
                input_weight,
                (own_grad,),
            )
            if tail:
                outs, feed.state = tie(outs, feed.state)
            to_diagonal, to_core, to_across, mine = outs
            from_diagonal = swap(to_diagonal, 1)
            from_core = swap(to_core, 1)
            pair = (to_across.astype(F32) + from_diagonal.astype(F32)).astype(BF16)
            pair_came = swap(pair, 2)
            after = pair
            if tail:
                after = start(feed, after)
            blocks, after = tie(blocks, after)
            in_pair = (blocks, (own_grad, both_grad))
            out_pair = (middle_blocks, (first[1], second[1]))
            parts = (mine, from_core, pair_came)
            if tail:
                digit = bits.digit([bits.seq[0]])
                halves = head_grads(
                    plan, me, digit, 2, (in_pair, out_pair), [heads[l] for l in range(1, layers)]
                )
                heads = Chain(bits, bits.seq, *halves)
                parts = start(heads, parts)
            else:
                (heads[layer],) = head_grads(plan, me, zero, 1, (in_pair, out_pair))
                parts, heads[layer] = tie(parts, heads[layer])
            carry, sums[layer] = carry_back(
                plan,
                layer,
                me,
                env_row,
                envs,
                parts,
                stream,
                middle_grad,
                norm_gain,
                [] if layer else [*last_sums] + [s for l in range(1, layers) for s in sums[l]],
                True,
            )
            if layer:
                sums[layer] = (*last_sums, sums[layer])
        small = sums[0]
        if by_steps:
            for step in small_steps(bits)[:CUT]:
                small = start(feed, small)
                small = start(heads, small)
                small = sum_small(bits, step, small)
            for chain in (feed, heads):
                chain.state, small = tie(chain.state, small)
                chain.work()
            held["chains"] = [feed, heads]
            return carry, small, [feed.state, heads.state]
        small, feed = lax.psum((small, feed), ("seq", "head"))
        heads = lax.psum(jnp.concatenate([heads[l] for l in range(layers)], axis=1), "seq")
        return carry, small, [list(feed), [heads]]

    assert layers == 2
    middle_grad, middle_low, core, across, feed, *last_sums = feed_back(last, carry)
    feed_total = lax.psum(feed, ("seq", "head"))
    own_grad = own_back(last, middle_low, core)
    across, own_grad = tie(across, own_grad)
    state = (middle_grad, middle_low, core, across, own_grad, tuple(last_sums))
    shapes = jax.eval_shape(finish, state)
    carry, small, states = lax.cond(
        frame_mask[0, 0, 0] > 0,
        finish,
        lambda _: jax.tree.map(lambda s: jnp.zeros(s.shape, s.dtype), shapes),
        state,
    )
    states, small, feed_total = tie(states, small, feed_total)
    two = jnp.zeros((2,), jnp.int32)
    if by_steps:
        feed, heads = held["chains"]
        for chain, state in zip((feed, heads), states):
            chain.state = list(state)
        rest = small_steps(bits)[CUT:]
        filled = None
        while feed.at > 1:
            feed.exchange()
            if not heads.done:
                heads.exchange()
            if rest:
                small = sum_small(bits, rest.pop(0), small)
            elif filled is None:
                filled = emit_feed(plan, zero, two, last, layers, feed_total, ())
            feed.state, filled, small = tie(feed.state, filled, small)
            feed.work()
            if not heads.done:
                feed.state, heads.state = tie(feed.state, heads.state)
                heads.work()
        mine = feed.state[0]
        came = bits.send(mine, [feed_plan[1]], 1)
        from_core = bits.send(mine, [bits.core], 1)
        if not heads.done:
            heads.exchange()
        if filled is None:
            filled = emit_feed(plan, zero, two, last, layers, feed_total, ())
        came, filled = tie(came, filled)
        also_core = bits.send(came, [bits.core], 1)
        while not heads.done:
            heads.work()
            heads.exchange()
        digits = jnp.concatenate([bits.bit(mask) for mask in feed_plan[1]])
        sources = [mine, came, from_core, also_core]
        feed_out = emit_feed(plan, me, digits, 0, layers, sources, filled)
        digit = bits.digit([bits.seq[0]])
        heads = heads.state
    else:
        filled = emit_feed(plan, zero, two, last, layers, feed_total, ())
        feed, heads = states
        feed_out = emit_feed(plan, zero, two, 0, layers, feed, filled)
        digit = zero
    head_out = emit_heads(plan, digit, layers, heads)
    environment_total, gain_out, shift_out, out_bias_out, up_bias_out, down_bias_out = emit_small(
        plan, layers, envs, small
    )
    return (
        mixed,
        carry,
        environment_total,
        gain_out,
        shift_out,
        head_out[0],
        head_out[1],
        out_bias_out,
        feed_out[0],
        up_bias_out,
        feed_out[1],
        down_bias_out,
    )


def solution(mesh):
    return jax.shard_map(
        body,
        mesh=mesh,
        in_specs=(
            P(("seq", "head"), None),
            P("seq", None, None),
            P("seq", None),
            P("seq", None, None),
            P("seq"),
            P(),
            P(),
            P(),
            P(None, None, None, "head"),
            P(None, "head", None),
            P(),
            P(),
            P(),
            P(),
            P(),
            P(("seq", "head"), None),
        ),
        out_specs=(
            P(("seq", "head"), None),
            P(("seq", "head"), None),
            P(),
            P(),
            P(),
            P(None, None, None, "head"),
            P(None, "head", None),
            P(),
            P(),
            P(),
            P(),
            P(),
        ),
        check_vma=False,
    )
```

```python
import functools
import math

import jax
import jax.numpy as jnp
from jax import lax
from jax.experimental import pallas as pl
from jax.experimental.pallas import tpu as pltpu
from jax.sharding import PartitionSpec as P

HEAD_DIM = 64
EPSILON = 1e-05
MASKED = -1e30
LOG2E = math.log2(math.e)
LN2 = math.log(2.0)
LANES = 128
BF16 = jnp.bfloat16
F32 = jnp.float32
NT = (((1,), (1,)), ((), ()))
NN = (((1,), (0,)), ((), ()))
TN = (((0,), (0,)), ((), ()))
MIB = 1024 * 1024
SMEM = pltpu.MemorySpace.SMEM


def up_to(value, step):
    return -(-value // step) * step


def dot(a, b, dims=NN):
    return lax.dot_general(a, b, dims, preferred_element_type=F32)


class Plan:
    def __init__(self, rows, groups, seqs, frames, width, local_width, hidden):
        self.rows, self.groups, self.seqs, self.frames = rows, groups, seqs, frames
        self.width, self.local, self.hidden = width, local_width, hidden
        self.block = up_to(rows, 16)
        self.total = self.block * groups
        self.length = rows * groups // seqs
        self.patches = self.length // frames
        self.heads = local_width // HEAD_DIM
        self.group_lanes = LANES // self.heads
        place = lambda t: t // rows * self.block + t % rows
        starts = [place(s * self.length) // 16 * 16 for s in range(seqs)]
        ends = [place((s + 1) * self.length - 1) + 1 for s in range(seqs)]
        self.window = max(up_to(e - s, 16) for s, e in zip(starts, ends))
        self.stride = starts[1] - starts[0]
        assert seqs == 3 and groups == 4
        assert starts == [self.stride * s for s in range(seqs)]
        assert self.window <= 2 * self.block
        assert starts[-1] + self.window <= self.total
        self.lanes = up_to(self.window, LANES)
        first = [
            min(place(s * self.length + f * self.patches) - starts[s] for s in range(seqs))
            for f in range(frames)
        ]
        last = [
            max(
                place(s * self.length + (f + 1) * self.patches - 1) - starts[s] + 1
                for s in range(seqs)
            )
            for f in range(frames)
        ]
        self.cuts = [first[f] // 16 * 16 if f else 0 for f in range(frames)] + [self.window]
        ends = [0] + [min(up_to(last[f], LANES), self.lanes) for f in range(frames - 1)] + [self.lanes]
        self.key_chunks = [
            (ends[f], ends[f + 1] - ends[f], self.cuts[f]) for f in range(frames)
        ]
        begins = [first[f] // LANES * LANES if f else 0 for f in range(frames)] + [self.lanes]
        reach = [up_to(last[f], 16) for f in range(frames - 1)] + [self.window]
        self.query_chunks = [
            (begins[f], begins[f + 1] - begins[f], reach[f]) for f in range(frames)
        ]

    def sequence(self, slot, across):
        if slot == 2:
            return 1
        return across * (self.seqs - 1) if slot == 0 else (1 - across) * (self.seqs - 1)


def params(mib):
    return pltpu.CompilerParams(vmem_limit_bytes=mib * MIB)


def result(shape, dtype, away=False):
    return pltpu.HBM(shape, dtype) if away else jax.ShapeDtypeStruct(shape, dtype)


def far(arrays, away=True):
    return [pltpu.with_memory_space_constraint(a, pltpu.HBM) if away else a for a in arrays]


def cost(microseconds):
    return pl.CostEstimate(flops=0, bytes_accessed=int(3.69e6 * microseconds), transcendentals=0)


def full(shape):
    return pl.BlockSpec(shape, lambda *i: (0,) * len(shape))


def layer_of(shape, layer):
    return pl.BlockSpec((None,) + shape, lambda *i: (layer,) + (0,) * len(shape))


def norm_stats(values):
    center = values - jnp.mean(values, axis=-1, keepdims=True)
    spread = jnp.mean(center * center, axis=-1, keepdims=True)
    return center, lax.rsqrt(spread + EPSILON)


def norm_back(upstream, center, scale, gain):
    unit = center * scale
    weighted = upstream * gain
    mean_w = jnp.mean(weighted, axis=-1, keepdims=True)
    mean_wn = jnp.mean(weighted * unit, axis=-1, keepdims=True)
    grad = scale * (weighted - mean_w - unit * mean_wn)
    return (
        grad,
        jnp.sum(upstream * unit, axis=0, keepdims=True),
        jnp.sum(upstream, axis=0, keepdims=True),
    )


def prologue_kernel(
    plan, me_ref, act_mask, frame_mask, env_id, tokens, actions, embed, gain, shift, stream, normed, qhot, kbias, valid
):
    rows, block = plan.rows, plan.block
    row = lax.broadcasted_iota(jnp.int32, (block, plan.width), 0)
    place = me_ref[0] * rows + row
    condition = jnp.zeros((block, plan.width), F32)
    for s in range(plan.seqs):
        env = jnp.zeros((1, plan.width), F32)
        for e in range(embed.shape[0]):
            env = jnp.where(env_id[0:1, s : s + 1] == e, embed[e : e + 1, :], env)
        for f in range(plan.frames):
            mask = act_mask[s : s + 1, f : f + 1].astype(F32)
            term = actions[s, f : f + 1, :].astype(F32) * mask + env
            begin = s * plan.length + f * plan.patches
            condition = jnp.where(
                (place >= begin) & (place < begin + plan.patches), term, condition
            )
    padded = jnp.concatenate(
        [tokens[...].astype(F32), jnp.zeros((block - rows, plan.width), F32)], axis=0
    )
    values = jnp.where(row < rows, padded + condition, 0.0)
    stream[...] = values
    center, scale = norm_stats(values)
    normed[...] = (center * scale * gain[0:1, :] + shift[0:1, :]).astype(BF16)
    line = lax.broadcasted_iota(jnp.int32, (plan.lanes, LANES), 0)
    lane = lax.broadcasted_iota(jnp.int32, (plan.lanes, LANES), 1) % plan.group_lanes
    for slot in range(plan.seqs):
        s = plan.sequence(slot, me_ref[0] // 2)
        at = plan.stride * s + line
        origin = at
        inside = line < plan.window
        for b in range(plan.groups):
            here = (at >= b * block) & (at < (b + 1) * block)
            origin = jnp.where(here, at - b * (block - rows), origin)
            inside = inside & jnp.logical_not(here & (at >= b * block + rows))
        token = origin - s * plan.length
        inside = inside & (token >= 0) & (token < plan.length)
        frame = jnp.zeros_like(token)
        for f in range(1, plan.frames):
            frame = frame + jnp.where(token >= f * plan.patches, 1, 0)
        frame = jnp.where(inside, frame, -1)
        qhot[slot] = jnp.where((lane == frame) & inside, 1.0, 0.0).astype(BF16)
        valid[slot] = jnp.where(inside, 1.0, 0.0)[: plan.window].astype(BF16)
        bias = jnp.where(lane < plan.frames, MASKED, 0.0)
        bias = jnp.where((lane >= plan.frames) & (lane < plan.frames + 3), 1.0, bias)
        allowed = frame_mask[s]
        for f in range(plan.frames):
            for g in range(plan.frames):
                value = jnp.where(allowed[f : f + 1, g : g + 1] > 0, 0.0, MASKED)
                bias = jnp.where((lane == f) & (frame == g), value, bias)
        kbias[slot] = bias.astype(BF16)


def prologue(plan, me, action_mask, frame_mask, env_id, tokens, actions, embed, gain, shift):
    return pl.pallas_call(
        functools.partial(prologue_kernel, plan),
        grid=(1,),
        in_specs=[pl.BlockSpec(memory_space=SMEM)]
        + [full(action_mask.shape), full(frame_mask.shape), full(env_id.shape)]
        + [full(tokens.shape), full(actions.shape), full(embed.shape)]
        + [layer_of(gain.shape[1:], 0), layer_of(gain.shape[1:], 0)],
        out_specs=[
            full((plan.block, plan.width)),
            full((plan.block, plan.width)),
            full((plan.seqs, plan.lanes, LANES)),
            full((plan.seqs, plan.lanes, LANES)),
            full((plan.seqs, plan.window, LANES)),
        ],
        out_shape=[
            jax.ShapeDtypeStruct((plan.block, plan.width), F32),
            jax.ShapeDtypeStruct((plan.block, plan.width), BF16),
            result((plan.seqs, plan.lanes, LANES), BF16),
            result((plan.seqs, plan.lanes, LANES), BF16),
            result((plan.seqs, plan.window, LANES), BF16),
        ],
        compiler_params=params(16),
        cost_estimate=cost(5),
        name="prologue",
    )(me, *far([action_mask, frame_mask, env_id, tokens, actions, embed, gain, shift]))


def place_blocks(plan, me, blocks, target):
    x, c = me[0] // 2, me[0] % 2
    if len(blocks) == 2:
        order = [c, 1 - c]
    else:
        order = [2 * x + c, 2 * x + 1 - c, 2 * (1 - x) + c, 2 * (1 - x) + 1 - c]
    for ref, b in zip(blocks, order):
        target[pl.ds(pl.multiple_of(b * plan.block, 16), plan.block), :] = ref[...]


def scatter_blocks(plan, me, block_of, outs):
    x, c = me[0] // 2, me[0] % 2
    order = [2 * (1 - x) + 1 - c, 2 * x + 1 - c, 2 * (1 - x) + c, 2 * x + c]
    for ref, b in zip(outs, order):
        rows = pl.ds(pl.multiple_of(b * plan.block, 16), plan.block)
        ref[...] = block_of(rows).astype(BF16)


def window_start(plan, me, slots, blocks):
    x = me[0] // 2
    if len(slots) == 1:
        s = plan.sequence(slots[0], x)
    else:
        s = jnp.int32(0)
        for i, slot in enumerate(slots):
            s = jnp.where(pl.program_id(0) == i, plan.sequence(slot, x), s)
    start = s * plan.stride
    if blocks == 2:
        start = start - x * (2 * plan.block)
    return pl.multiple_of(start, 16)


def group_mask(plan, head):
    lane = lax.broadcasted_iota(jnp.int32, (1, LANES), 1)
    return jnp.where(lane // plan.group_lanes == head, 1.0, 0.0).astype(BF16)


def put_windows(plan, me, slots, before, target, value):
    over = plan.window - plan.stride
    step = pl.program_id(0)
    at = window_start(plan, me, slots, 4)

    @pl.when(step == 0)
    def _():
        target[...] = jnp.zeros(target.shape, target.dtype)
        for slot, ref in enumerate(before):
            start = pl.multiple_of(plan.sequence(slot, me[0] // 2) * plan.stride, 16)
            target[pl.ds(start, plan.window), :] = ref[0]

    inner = pl.ds(pl.multiple_of(at + over, 16), plan.window - 2 * over)
    target[inner, :] = value[over : plan.window - over]
    for begin in (0, plan.window - over):
        rows = pl.ds(pl.multiple_of(at + begin, 16), over)
        target[rows, :] = target[rows, :] + value[begin : begin + over]


def attend_kernel(plan, slots, blocks, *refs):
    me, refs = refs[0], refs[1:]
    placed, refs = refs[:blocks], refs[blocks:]
    w_in, qhot, kbias, valid = refs[:4]
    refs = refs[4:]
    last = blocks == 4
    if last:
        w_out, before, refs = refs[0], refs[1], refs[2:]
    triple, attention, lse = refs[:3]
    refs = refs[3:]
    if last:
        outs, refs = refs[:4], refs[4:]
    gathered, q_even, q_odd, keys, values, *whole = refs
    window, local = plan.window, plan.local

    @pl.when(pl.program_id(0) == 0)
    def _():
        place_blocks(plan, me, placed, gathered)
        keys[window:, :] = jnp.zeros((plan.lanes - window, local), BF16)
        values[window:, :] = jnp.zeros((plan.lanes - window, local), BF16)

    x = gathered[pl.ds(window_start(plan, me, slots, blocks), window), :]
    query = dot(x, w_in[0]) * (HEAD_DIM ** (-0.5) * LOG2E)
    odd_lane = lax.broadcasted_iota(jnp.int32, (1, local), 1) // HEAD_DIM % 2 == 1
    q_even[...] = jnp.where(odd_lane, 0.0, query).astype(BF16)
    q_odd[...] = jnp.where(odd_lane, query, 0.0).astype(BF16)
    triple[0, :, 0:local] = query.astype(BF16)
    key = dot(x, w_in[1]).astype(BF16)
    triple[0, :, local : 2 * local] = key
    keys[0:window, :] = key
    value = dot(x, w_in[2]).astype(BF16)
    triple[0, :, 2 * local : 3 * local] = value
    values[0:window, :] = value
    left = lax.broadcasted_iota(jnp.int32, (1, LANES), 1) < HEAD_DIM
    lane_head = lax.broadcasted_iota(jnp.int32, (1, LANES), 1) // plan.group_lanes
    chunks = plan.key_chunks
    spans = list(zip(plan.cuts[:-1], plan.cuts[1:]))

    def scores_of(head):
        cols = slice(head // 2 * LANES, (head // 2 + 1) * LANES)
        q = (q_even, q_odd)[head % 2]
        pick = group_mask(plan, head)
        scores = []
        for k0, count, r0 in chunks:
            lhs = jnp.concatenate([q[r0:, cols], qhot[0, r0:window, :]], axis=1)
            rhs = jnp.concatenate(
                [keys[k0 : k0 + count, cols], kbias[0, k0 : k0 + count, :] * pick], axis=1
            )
            scores.append(dot(lhs, rhs, NT))
        return scores

    def soften(scores):
        tops, weights = [], [[] for _ in chunks]
        for i, (begin, end) in enumerate(spans):
            pieces = [scores[c][begin - chunks[c][2] : end - chunks[c][2]] for c in range(i + 1)]
            top = jnp.max(jnp.concatenate(pieces, axis=1), axis=-1, keepdims=True)
            tops.append(jnp.broadcast_to(top, (end - begin, LANES)))
            for c in range(i + 1):
                weights[c].append(jnp.exp2(pieces[c] - top).astype(BF16))
        return jnp.concatenate(tops, axis=0), [jnp.concatenate(w, axis=0) for w in weights]

    def mix(head, weights):
        cols = slice(head // 2 * LANES, (head // 2 + 1) * LANES)
        parts = []
        for (k0, count, _), weight in zip(chunks, weights):
            rhs = jnp.concatenate(
                [values[k0 : k0 + count, cols], jnp.ones((count, LANES), BF16)], axis=1
            )
            parts.append(dot(weight, rhs))
        rows = []
        for i, (begin, end) in enumerate(spans):
            pieces = [parts[c][begin - chunks[c][2] : end - chunks[c][2]] for c in range(i + 1)]
            rows.append(functools.reduce(jnp.add, pieces))
        return jnp.concatenate(rows, axis=0)

    state = {}

    def finish(head, top, mixed):
        total = mixed[:, LANES:]
        state[head] = mixed[:, :LANES] / total
        if head == 0:
            state["top"], state["total"] = top, total
        else:
            state["top"] = jnp.where(lane_head == head, top, state["top"])
            state["total"] = jnp.where(lane_head == head, total, state["total"])
        if head % 2 == 1:
            both = jnp.where(left, state[head - 1], state[head]) * valid[0].astype(F32)
            attention[0, :, (head // 2) * LANES : (head // 2 + 1) * LANES] = both.astype(BF16)

    heads = plan.heads
    scores = {h: scores_of(h) for h in range(min(2, heads))}
    soft, mixed = {}, {}
    for h in range(heads):
        soft[h] = soften(scores.pop(h))
        if h + 2 < heads:
            scores[h + 2] = scores_of(h + 2)
        mixed[h] = mix(h, soft[h][1])
        if h >= 1:
            finish(h - 1, soft[h - 1][0], mixed.pop(h - 1))
    finish(heads - 1, soft[heads - 1][0], mixed.pop(heads - 1))
    lse[0] = state["top"] + jnp.log2(state["total"])
    if last:
        put_windows(plan, me, slots, [before], whole[0], attention[0])

        @pl.when(pl.program_id(0) == len(slots) - 1)
        def _():
            scatter_blocks(plan, me, lambda rows: dot(whole[0][rows, :], w_out[...]), outs)


def per_slot(slots, shape):
    first = slots[0]
    return pl.BlockSpec((1,) + shape, lambda s: (s + first,) + (0,) * len(shape))


def attend(plan, layer, slots, me, blocks, input_weight, masks, away, output_weight=None, before=None):
    block = (plan.block, plan.width)
    n = len(slots)
    last = before is not None
    each = lambda shape: pl.BlockSpec((1,) + shape, lambda s: (s, 0, 0))
    shape = lambda *dims: result((n, plan.window) + dims, BF16, away)
    in_specs = [pl.BlockSpec(memory_space=SMEM)] + [full(block)] * len(blocks)
    in_specs += [layer_of(input_weight.shape[1:], layer)]
    in_specs += [per_slot(slots, m.shape[1:]) for m in masks]
    out_specs = [
        each((plan.window, 3 * plan.local)),
        each((plan.window, plan.local)),
        each((plan.window, LANES)),
    ]
    out_shape = [
        shape(3 * plan.local),
        shape(plan.local),
        result((n, plan.window, LANES), F32, away),
    ]
    scratch = [
        pltpu.VMEM((len(blocks) * plan.block, plan.width), BF16),
        pltpu.VMEM((plan.window, plan.local), BF16),
        pltpu.VMEM((plan.window, plan.local), BF16),
        pltpu.VMEM((plan.lanes, plan.local), BF16),
        pltpu.VMEM((plan.lanes, plan.local), BF16),
    ]
    args = [me, *blocks, input_weight, *masks]
    if last:
        in_specs += [layer_of(output_weight.shape[1:], layer), full(before.shape)]
        args += [output_weight, before]
        out_specs += [full(block)] * 4
        out_shape += [jax.ShapeDtypeStruct(block, BF16)] * 4
        scratch += [pltpu.VMEM((plan.total, plan.local), BF16)]
    area = plan.window * plan.lanes * plan.heads
    return pl.pallas_call(
        functools.partial(attend_kernel, plan, slots, len(blocks)),
        grid=(n,),
        in_specs=in_specs,
        out_specs=out_specs,
        out_shape=out_shape,
        scratch_shapes=scratch,
        compiler_params=params(20),
        cost_estimate=cost(3 * n),
        name="attend",
    )(*args)


def three_parts(value):
    high = value.astype(BF16)
    rest = value - high.astype(F32)
    middle = rest.astype(BF16)
    low = (rest - middle.astype(F32)).astype(BF16)
    return high.astype(F32), middle.astype(F32), low.astype(F32)


def attend_back_kernel(plan, slots, blocks, *refs):
    me, refs = refs[0], refs[1:]
    placed, refs = refs[:blocks], refs[blocks:]
    w_out, qhot, kbias, valid, triple, attention, lse = refs[:7]
    refs = refs[7:]
    last = slots[-1] == plan.seqs - 1
    if last:
        w_in, before, refs = refs[0], refs[1 : 1 + slots[0]], refs[1 + slots[0] :]
    triple_grad, refs = refs[0], refs[1:]
    if last:
        outs, refs = refs[:4], refs[4:]
    gathered, queries, grads, query_side, grad_side, key_turned, *whole = refs
    window, local, lanes = plan.window, plan.local, plan.lanes

    @pl.when(pl.program_id(0) == 0)
    def _():
        place_blocks(plan, me, placed, gathered)
        queries[window:, :] = jnp.zeros((lanes - window, local), BF16)
        grads[window:, :] = jnp.zeros((lanes - window, local), BF16)
        query_side[window:, :] = jnp.zeros((lanes - window, LANES), BF16)
        grad_side[window:, :] = jnp.zeros((lanes - window, LANES), BF16)

    mask = valid[0].astype(F32)
    head_grad = dot(gathered[pl.ds(window_start(plan, me, slots, blocks), window), :], w_out[...], NT)
    head_grad = head_grad * jnp.concatenate([mask] * (local // LANES), axis=1)
    head_grad = head_grad.astype(BF16)
    grads[0:window, :] = head_grad
    queries[0:window, :] = triple[0, :, 0:local]
    key_turned[...] = triple[0, :, local : 2 * local].T
    product = head_grad.astype(F32) * attention[0].astype(F32)
    high = product.astype(BF16)
    low = (product - high.astype(F32)).astype(BF16)
    spread = jnp.where(
        lax.broadcasted_iota(jnp.int32, (local, LANES), 0) // HEAD_DIM
        == lax.broadcasted_iota(jnp.int32, (local, LANES), 1) // plan.group_lanes,
        1.0,
        0.0,
    ).astype(BF16)
    inner = dot(high, spread) + dot(low, spread)
    slot = lax.broadcasted_iota(jnp.int32, (1, LANES), 1) % plan.group_lanes
    a, b, c = three_parts(-inner)
    grad_side[0:window, :] = jnp.where(
        slot == 0, a, jnp.where(slot == 1, b, jnp.where(slot == 2, c, 0.0))
    ).astype(BF16)
    a, b, c = three_parts(-lse[0])
    n = plan.frames
    query_side[0:window, :] = jnp.where(
        slot < n,
        qhot[0, 0:window, :].astype(F32),
        jnp.where(slot == n, a, jnp.where(slot == n + 1, b, jnp.where(slot == n + 2, c, 0.0))),
    ).astype(BF16)
    left = lax.broadcasted_iota(jnp.int32, (1, LANES), 1) < HEAD_DIM
    sides = [jnp.where(left, 1.0, 0.0).astype(BF16), jnp.where(left, 0.0, 1.0).astype(BF16)]
    chunks = plan.query_chunks
    ends = [0] + [c[2] for c in chunks]

    def products(head):
        half = head % 2
        tile = head // 2 * LANES
        cols = slice(tile, tile + LANES)
        pick = group_mask(plan, head)
        ones = jnp.where(slot < 3, pick.astype(F32), 0.0).astype(BF16)
        key_side = jnp.concatenate(
            [
                triple[0, :, local + tile : local + tile + LANES] * sides[half],
                kbias[0, 0:window, :] * pick,
            ],
            axis=1,
        )
        value_side = jnp.concatenate(
            [
                triple[0, :, 2 * local + tile : 2 * local + tile + LANES] * sides[half],
                jnp.broadcast_to(ones, (window, LANES)),
            ],
            axis=1,
        )
        scores, prob_grads = [], []
        for q0, count, reach in chunks:
            rows = slice(q0, q0 + count)
            rhs = jnp.concatenate([queries[rows, cols], query_side[rows, :]], axis=1)
            scores.append(dot(key_side[:reach], rhs, NT))
        for q0, count, reach in chunks:
            rows = slice(q0, q0 + count)
            rhs = jnp.concatenate([grads[rows, cols], grad_side[rows, :]], axis=1)
            prob_grads.append(dot(value_side[:reach], rhs, NT))
        return scores, prob_grads

    def pointwise(scores, prob_grads):
        probs = [jnp.exp2(s) for s in scores]
        score_grads = [(p * g).astype(BF16) for p, g in zip(probs, prob_grads)]
        return [p.astype(BF16) for p in probs], score_grads

    def add_rows(parts):
        rows = []
        for i in range(len(chunks)):
            pieces = [p[ends[i] : ends[i + 1]] for p in parts[i:]]
            rows.append(functools.reduce(jnp.add, pieces))
        return jnp.concatenate(rows, axis=0)

    def gradients(head, probs, score_grads):
        tile = head // 2 * LANES
        cols = slice(tile, tile + LANES)
        value_parts, key_parts, query_parts = [], [], []
        turned = key_turned[tile + head % 2 * HEAD_DIM : tile + (head % 2 + 1) * HEAD_DIM, :]
        for (q0, count, reach), prob in zip(chunks, probs):
            value_parts.append(dot(prob, grads[q0 : q0 + count, cols]))
        for (q0, count, reach), score_grad in zip(chunks, score_grads):
            key_parts.append(dot(score_grad, queries[q0 : q0 + count, cols]))
        for (q0, count, reach), score_grad in zip(chunks, score_grads):
            query_parts.append(dot(turned[:, :reach], score_grad))
        return jnp.concatenate(query_parts, axis=1), add_rows(key_parts), add_rows(value_parts)

    heads = plan.heads
    found = [products(h) for h in range(heads)]
    pointed = [pointwise(*f) for f in found]
    for tile in range(heads // 2):
        even, odd = (gradients(h, *pointed[h]) for h in (2 * tile, 2 * tile + 1))
        query = jnp.concatenate([even[0], odd[0]], axis=0).T[:window] * HEAD_DIM ** (-0.5)
        key = jnp.where(left, even[1], odd[1]) * LN2
        value = jnp.where(left, even[2], odd[2])
        for t, grad in enumerate((query, key, value)):
            at = t * local + tile * LANES
            triple_grad[0, :, at : at + LANES] = grad.astype(BF16)
    if last:
        put_windows(plan, me, slots, before, whole[0], triple_grad[0])

        @pl.when(pl.program_id(0) == len(slots) - 1)
        def _():
            def back(rows):
                total = dot(whole[0][rows, 0:local], w_in[0], NT)
                for t in (1, 2):
                    total = total + dot(whole[0][rows, t * local : (t + 1) * local], w_in[t], NT)
                return total

            scatter_blocks(plan, me, back, outs)


def attend_back(plan, layer, slots, me, blocks, output_weight, masks, saved, away, input_weight=None, before=None):
    block = (plan.block, plan.width)
    n = len(slots)
    last = before is not None
    each = lambda shape: pl.BlockSpec((1,) + shape, lambda s: (s, 0, 0))
    in_specs = [pl.BlockSpec(memory_space=SMEM)] + [full(block)] * len(blocks)
    in_specs += [layer_of(output_weight.shape[1:], layer)]
    in_specs += [per_slot(slots, m.shape[1:]) for m in masks]
    in_specs += [per_slot([max(slots[0] - 1, 0)], a.shape[1:]) for a in saved]
    out_specs = [each((plan.window, 3 * plan.local))]
    out_shape = [jax.ShapeDtypeStruct((n, plan.window, 3 * plan.local), BF16)]
    scratch = [
        pltpu.VMEM((len(blocks) * plan.block, plan.width), BF16),
        pltpu.VMEM((plan.lanes, plan.local), BF16),
        pltpu.VMEM((plan.lanes, plan.local), BF16),
        pltpu.VMEM((plan.lanes, LANES), BF16),
        pltpu.VMEM((plan.lanes, LANES), BF16),
        pltpu.VMEM((plan.local, plan.window), BF16),
    ]
    args = [me, *blocks, *far([output_weight, *masks, *saved])]
    if last:
        in_specs += [layer_of(input_weight.shape[1:], layer)] + [full(w.shape) for w in before]
        args += [*far([input_weight]), *before]
        out_specs += [full(block)] * 4
        out_shape += [jax.ShapeDtypeStruct(block, BF16)] * 4
        scratch += [pltpu.VMEM((plan.total, 3 * plan.local), BF16)]
    area = plan.window * plan.lanes * plan.heads
    return pl.pallas_call(
        functools.partial(attend_back_kernel, plan, slots, len(blocks)),
        grid=(n,),
        in_specs=in_specs,
        out_specs=out_specs,
        out_shape=out_shape,
        scratch_shapes=scratch,
        compiler_params=params(28),
        cost_estimate=cost(6 * n),
        name="attend_back",
    )(*args)


FF_STEPS = 4


def forward_kernel(plan, last, stream, part_a, part_b, part_c, out_bias, gain, shift, up, up_bias, down, down_bias, next_gain, next_shift, middle, lifted, hidden, slope, *rest):
    outs, total = rest[:-1], rest[-1]
    step = pl.program_id(0)

    @pl.when(step == 0)
    def _():
        projected = part_a[...].astype(F32) + part_b[...].astype(F32) + part_c[...].astype(F32)
        values = stream[...] + (projected + out_bias[...])
        middle[...] = values
        center, scale = norm_stats(values)
        lifted[...] = (center * scale * gain[1:2, :] + shift[1:2, :]).astype(BF16)
        total[...] = values + down_bias[...]

    before = dot(lifted[...], up[...]) + up_bias[...]
    cdf = 0.5 + 0.5 * lax.erf(before * (2.0**-0.5))
    density = jnp.exp2(before * before * (-0.5 * LOG2E)) * (2.0 * math.pi) ** -0.5
    act = (before * cdf).astype(BF16)
    hidden[...] = act
    slope[...] = (cdf + before * density).astype(BF16)
    total[...] += dot(act, down[...])

    @pl.when(step == FF_STEPS - 1)
    def _():
        values = total[...]
        if last:
            outs[0][...] = values.astype(BF16)[: plan.rows]
        else:
            outs[0][...] = values
            center, scale = norm_stats(values)
            outs[1][...] = (center * scale * next_gain[0:1, :] + next_shift[0:1, :]).astype(BF16)


def forward_rest(plan, layer, layers, stream, parts, output_bias, gain, shift, up, up_bias, down, down_bias):
    last = layer == layers - 1
    block = (plan.block, plan.width)
    cols = plan.hidden // FF_STEPS
    follow = min(layer + 1, layers - 1)
    wide = pl.BlockSpec((plan.block, cols), lambda j: (0, j))
    row = lambda width: layer_of((1, width), layer)
    if last:
        tail_specs = [full((plan.rows, plan.width))]
        tail = [jax.ShapeDtypeStruct((plan.rows, plan.width), BF16)]
    else:
        tail_specs = [full(block), full(block)]
        tail = [jax.ShapeDtypeStruct(block, F32), jax.ShapeDtypeStruct(block, BF16)]
    return pl.pallas_call(
        functools.partial(forward_kernel, plan, last),
        grid=(FF_STEPS,),
        in_specs=[full(block)] * 4
        + [
            row(plan.width),
            layer_of(gain.shape[1:], layer),
            layer_of(gain.shape[1:], layer),
            pl.BlockSpec((None, plan.width, cols), lambda j: (layer, 0, j)),
            pl.BlockSpec((None, 1, cols), lambda j: (layer, 0, j)),
            pl.BlockSpec((None, cols, plan.width), lambda j: (layer, j, 0)),
            row(plan.width),
            layer_of(gain.shape[1:], follow),
            layer_of(gain.shape[1:], follow),
        ],
        out_specs=[full(block), full(block), wide, wide] + tail_specs,
        out_shape=[
            result(block, F32),
            result(block, BF16),
            result((plan.block, plan.hidden), BF16),
            result((plan.block, plan.hidden), BF16),
        ]
        + tail,
        scratch_shapes=[pltpu.VMEM(block, F32)],
        compiler_params=params(20),
        cost_estimate=cost(5),
        name="forward_rest",
    )(stream, *parts, *far([output_bias, gain, shift]), up, *far([up_bias]), down, *far([down_bias, gain, shift]))


def back_kernel(plan, carry, middle, slope, gain, up, down, low, before_low, middle_grad, middle_low, sums, up_bias, total):
    step = pl.program_id(0)

    @pl.when(step == 0)
    def _():
        low[...] = carry[...].astype(BF16)
        total[...] = jnp.zeros(total.shape, F32)

    before_grad = dot(low[...], down[...], NT) * slope[...].astype(F32)
    up_bias[...] = jnp.sum(before_grad, axis=0, keepdims=True)
    narrow = before_grad.astype(BF16)
    before_low[...] = narrow
    total[...] += dot(narrow, up[...], NT)

    @pl.when(step == FF_STEPS - 1)
    def _():
        center, scale = norm_stats(middle[...])
        grad, gain_sum, shift_sum = norm_back(total[...], center, scale, gain[1:2, :])
        carried = carry[...]
        grad = carried + grad
        middle_grad[...] = grad
        middle_low[...] = grad.astype(BF16)
        sums[...] = jnp.zeros(sums.shape, F32)
        sums[0:1, :] = gain_sum
        sums[1:2, :] = shift_sum
        sums[2:3, :] = jnp.sum(grad, axis=0, keepdims=True)
        sums[3:4, :] = jnp.sum(carried, axis=0, keepdims=True)


def back_rest(plan, layer, carry, middle, slope, gain, up, down, away):
    block = (plan.block, plan.width)
    cols = plan.hidden // FF_STEPS
    wide = pl.BlockSpec((plan.block, cols), lambda j: (0, j))
    return pl.pallas_call(
        functools.partial(back_kernel, plan),
        grid=(FF_STEPS,),
        in_specs=[
            full(block),
            full(block),
            wide,
            layer_of(gain.shape[1:], layer),
            pl.BlockSpec((None, plan.width, cols), lambda j: (layer, 0, j)),
            pl.BlockSpec((None, cols, plan.width), lambda j: (layer, j, 0)),
        ],
        out_specs=[
            full(block),
            wide,
            full(block),
            full(block),
            full((8, plan.width)),
            pl.BlockSpec((1, cols), lambda j: (0, j)),
        ],
        out_shape=[
            jax.ShapeDtypeStruct(block, BF16),
            jax.ShapeDtypeStruct((plan.block, plan.hidden), BF16),
            jax.ShapeDtypeStruct(block, F32),
            jax.ShapeDtypeStruct(block, BF16),
            jax.ShapeDtypeStruct((8, plan.width), F32),
            jax.ShapeDtypeStruct((1, plan.hidden), F32),
        ],
        scratch_shapes=[pltpu.VMEM(block, F32)],
        compiler_params=params(20),
        cost_estimate=cost(6),
        name="back_rest",
    )(carry, *far((middle, slope), away), *far((gain, up, down)))


SMALL_ROWS = 8
CUT = 4


def carry_kernel(plan, wide, me, env_id, part_a, part_b, part_c, stream, middle_grad, gain, *rest):
    others, outs = rest[: len(rest) - 2], rest[-2:]
    carry, sums = outs
    upstream = part_a[...].astype(F32) + part_b[...].astype(F32) + part_c[...].astype(F32)
    center, scale = norm_stats(stream[...])
    grad, gain_sum, shift_sum = norm_back(upstream, center, scale, gain[0:1, :])
    grad = middle_grad[...] + grad
    carry[...] = grad[: carry.shape[0]]
    sums[...] = jnp.zeros(sums.shape, F32)
    sums[0:1, :] = gain_sum
    sums[1:2, :] = shift_sum
    if not others:
        return
    row = lax.broadcasted_iota(jnp.int32, (plan.block, plan.width), 0)
    place = me[0] * plan.rows + row
    envs = sums.shape[0] - SMALL_ROWS * (1 + len(others))
    line = lax.broadcasted_iota(jnp.int32, (envs, plan.width), 0)
    total = jnp.zeros((envs, plan.width), F32)
    for s in range(plan.seqs):
        inside = (row < plan.rows) & (place >= s * plan.length)
        inside = inside & (place < (s + 1) * plan.length)
        part = jnp.sum(jnp.where(inside, grad, 0.0), axis=0, keepdims=True)
        total = total + jnp.where(line == env_id[0:1, s : s + 1], part, 0.0)
    at = SMALL_ROWS
    for ref in others:
        if ref.shape[0] == 1:
            for i in range(SMALL_ROWS):
                sums[at + i : at + i + 1, 0:wide] = ref[:, i * wide : (i + 1) * wide]
        else:
            sums[at : at + SMALL_ROWS, :] = ref[...]
        at += SMALL_ROWS
    sums[at : at + envs, :] = total


def carry_back(plan, layer, me, env_id, envs, parts, stream, middle_grad, gain, others, away):
    block = (plan.block, plan.width)
    first = layer == 0
    rows = plan.rows if first else plan.block
    wide = plan.hidden // SMALL_ROWS
    assert wide <= plan.width and wide % LANES == 0
    small = SMALL_ROWS * (1 + len(others)) + (envs if first else 0)
    return pl.pallas_call(
        functools.partial(carry_kernel, plan, wide),
        grid=(1,),
        in_specs=[pl.BlockSpec(memory_space=SMEM), full(env_id.shape)]
        + [full(block)] * 5
        + [layer_of(gain.shape[1:], layer)]
        + [full(o.shape) for o in others],
        out_specs=[full((rows, plan.width)), full((small, plan.width))],
        out_shape=[
            jax.ShapeDtypeStruct((rows, plan.width), F32),
            jax.ShapeDtypeStruct((small, plan.width), F32),
        ],
        compiler_params=params(16),
        cost_estimate=cost(2),
        name="carry_back",
    )(me, *far([env_id]), *parts, *far([stream], away), middle_grad, *far([gain, *others]))


def emit_small_kernel(plan, layers, envs, small, env, gain, shift, out_bias, up_bias, down_bias):
    wide = plan.hidden // SMALL_ROWS
    at = SMALL_ROWS
    for layer in range(layers):
        second = at
        up = at + SMALL_ROWS
        first = 0 if layer == 0 else at + 2 * SMALL_ROWS
        at += (2 if layer == 0 else 3) * SMALL_ROWS
        gain[layer, 0:1, :] = small[first : first + 1, :]
        shift[layer, 0:1, :] = small[first + 1 : first + 2, :]
        gain[layer, 1:2, :] = small[second : second + 1, :]
        shift[layer, 1:2, :] = small[second + 1 : second + 2, :]
        out_bias[layer : layer + 1, :] = small[second + 2 : second + 3, :]
        down_bias[layer : layer + 1, :] = small[second + 3 : second + 4, :]
        for i in range(SMALL_ROWS):
            up_bias[layer : layer + 1, i * wide : (i + 1) * wide] = small[up + i : up + i + 1, 0:wide]
    env[...] = small[at : at + envs, :]


def emit_small(plan, layers, envs, small):
    shapes = [
        (envs, plan.width),
        (layers, 2, plan.width),
        (layers, 2, plan.width),
        (layers, plan.width),
        (layers, plan.hidden),
        (layers, plan.width),
    ]
    return pl.pallas_call(
        functools.partial(emit_small_kernel, plan, layers, envs),
        grid=(1,),
        in_specs=[full(small.shape)],
        out_specs=[full(s) for s in shapes],
        out_shape=[jax.ShapeDtypeStruct(s, F32) for s in shapes],
        compiler_params=params(8),
        cost_estimate=cost(1),
        name="emit_small",
    )(small)


def feed_grads_kernel(plan, me, lifted, before_low, low, hidden, keep, send, lifted_t, low_t):
    @pl.when(pl.program_id(0) == 0)
    def _():
        lifted_t[...] = lifted[...].T
        low_t[...] = low[...].T

    up = dot(lifted_t[...], before_low[...]).astype(BF16)
    down = dot(low_t[...], hidden[...]).astype(BF16)

    @pl.when(me[0] % 2 == 0)
    def _():
        keep[...] = up
        send[...] = down

    @pl.when(me[0] % 2 == 1)
    def _():
        keep[...] = down
        send[...] = up


def feed_grads(plan, me, lifted, before_low, low, hidden, away):
    block = (plan.block, plan.width)
    cols = plan.hidden // FF_STEPS
    wide = pl.BlockSpec((plan.block, cols), lambda j: (0, j))
    out = pl.BlockSpec((plan.width, cols), lambda j: (0, j))
    shape = result((plan.width, plan.hidden), BF16, True)
    return pl.pallas_call(
        functools.partial(feed_grads_kernel, plan),
        grid=(FF_STEPS,),
        in_specs=[pl.BlockSpec(memory_space=SMEM), full(block), wide, full(block), wide],
        out_specs=[out, out],
        out_shape=[shape, shape],
        scratch_shapes=[pltpu.VMEM((plan.width, plan.block), BF16)] * 2,
        compiler_params=params(16),
        cost_estimate=cost(5),
        name="feed_grads",
    )(me, *far([lifted], away), before_low, low, *far([hidden], away))


def head_grads_kernel(plan, kinds, beside, digit, *refs):
    me, refs = refs[0], refs[1:]
    scratch, refs = refs[-1], refs[:-1]
    columns = []
    for count in kinds:
        blocks, windows, refs = refs[:4], refs[4 : 4 + count], refs[4 + count :]
        place_blocks(plan, me, blocks, scratch)
        rights = [ref[i] for ref in windows for i in range(ref.shape[0])]
        total = None
        for slot, right in enumerate(rights):
            start = pl.multiple_of(plan.sequence(slot, me[0] // 2) * plan.stride, 16)
            part = dot(scratch[pl.ds(start, plan.window), :].T, right)
            total = part if total is None else total + part
        columns.append(total.astype(BF16))
    if beside:
        columns.append(refs[0][...])
        refs = refs[1:]
    value = jnp.concatenate(columns, axis=1) if len(columns) > 1 else columns[0]
    n = len(refs)
    if n == 1:
        refs[0][...] = value
        return
    count = plan.width // n
    for mine in range(n):

        @pl.when(digit[0] == mine)
        def _(mine=mine):
            for j, ref in enumerate(refs):
                at = (mine ^ j) * count
                ref[...] = value[at : at + count]


def head_grads(plan, me, digit, pieces, pairs, beside=()):
    cols = sum(p[1][0].shape[2] for p in pairs) + sum(b.shape[1] for b in beside)
    shape = (plan.width // pieces, cols)
    flat = [a for p in pairs for a in (*p[0], *p[1])] + list(beside)
    return pl.pallas_call(
        functools.partial(head_grads_kernel, plan, [len(p[1]) for p in pairs], len(beside)),
        grid=(1,),
        in_specs=[pl.BlockSpec(memory_space=SMEM)] * 2 + [full(a.shape) for a in flat],
        out_specs=[full(shape)] * pieces,
        out_shape=[jax.ShapeDtypeStruct(shape, BF16)] * pieces,
        scratch_shapes=[pltpu.VMEM((plan.total, plan.width), BF16)],
        compiler_params=params(20),
        cost_estimate=cost(5),
        name="head_grads",
    )(digit, me, *far(flat))


def swap(value, bit):
    size = lax.axis_size("head")
    return lax.ppermute(value, "head", [(i, i ^ bit) for i in range(size)])


def scatter(outs):
    to_diagonal, to_core, to_across, mine = outs
    first = swap(to_diagonal, 1)
    second = swap(to_core, 1)
    pair = (to_across.astype(F32) + first.astype(F32)).astype(BF16)
    return mine, second, swap(pair, 2)


def tie(*trees):
    return lax.optimization_barrier(trees)


class Bits:
    def __init__(self):
        self.heads = lax.axis_size("head")
        self.size = lax.axis_size("seq") * self.heads
        self.place = lax.axis_index("seq") * self.heads + lax.axis_index("head")
        self.place = self.place.astype(jnp.int32)
        seq = [self.heads << i for i in range((self.size // self.heads).bit_length() - 1)]
        self.core, self.across = (1, 1), (2, 2)
        self.seq = [(seq[0], seq[1]), (seq[1], seq[0])] + [(m, m) for m in seq[2:]]

    def bit(self, mask):
        return jnp.where((self.place & mask) > 0, 1, 0).astype(jnp.int32).reshape(1)

    def digit(self, step):
        core = self.place & 1
        value = jnp.int32(0)
        for i, (zero, one) in enumerate(step):
            mask = jnp.where(core == 0, zero, one)
            value = value + jnp.where((self.place & mask) > 0, 1 << i, 0)
        return value.astype(jnp.int32).reshape(1)

    def send(self, value, step, j):
        def partner(place):
            for i, masks in enumerate(step):
                if j >> i & 1:
                    place ^= masks[place & 1]
            return place

        pairs = [(p, partner(p)) for p in range(self.size)]
        return lax.ppermute(value, ("seq", "head"), pairs)


def cut(shape, pieces):
    if shape[0] % (16 * pieces) == 0:
        return 0
    if shape[1] % (LANES * pieces) == 0:
        return 1
    return None


def piece_at(shape, pieces, index):
    dim = cut(shape, pieces) if pieces > 1 else 0
    count = shape[dim] // pieces
    part = tuple(count if d == dim else shape[d] for d in range(2))
    if pieces == 1:
        return (slice(None), slice(None)), part
    window = pl.ds(pl.multiple_of(index * count, 16 if dim == 0 else LANES), count)
    return tuple(window if d == dim else slice(None) for d in range(2)), part


def fold_kernel(pieces, dim, digit, *refs):
    ins, outs = refs[: len(refs) - pieces], refs[len(refs) - pieces :]
    count = ins[0].shape[dim] // pieces
    for j, out in enumerate(outs):
        place = digit[0] ^ j if pieces > 1 else 0
        at = pl.ds(pl.multiple_of(place * count, LANES if dim else 16), count)
        where = (slice(None), at) if dim else (at, slice(None))
        total = ins[0][where].astype(F32)
        for ref in ins[1:]:
            total = total + ref[where].astype(F32)
        out[...] = total.astype(BF16)


def large(shape):
    return shape[0] * shape[1] >= 192 * 1024


def in_columns(shape, dim):
    return 1


def fold(digit, pieces, arrays):
    rows, cols = arrays[0].shape
    dim = cut((rows, cols), pieces)
    part = (rows, cols // pieces) if dim else (rows // pieces, cols)
    steps = in_columns((rows, cols), dim)
    of = lambda shape: pl.BlockSpec((shape[0], shape[1] // steps), lambda j: (0, j))
    return pl.pallas_call(
        functools.partial(fold_kernel, pieces, dim),
        grid=(steps,),
        in_specs=[pl.BlockSpec(memory_space=SMEM)] + [of((rows, cols))] * len(arrays),
        out_specs=[of(part)] * pieces,
        out_shape=[result(part, BF16, large(part))] * pieces,
        compiler_params=params(16),
        cost_estimate=cost(2 if large(arrays[0].shape) else 1),
        name="fold",
    )(digit, *far(arrays, large((rows, cols))))


def join_kernel(dim, digit, own, came, out):
    count = own.shape[dim]
    for j, ref in enumerate((own, came)):
        at = pl.ds(pl.multiple_of((digit[0] ^ j) * count, LANES if dim else 16), count)
        out[(slice(None), at) if dim else (at, slice(None))] = ref[...]


def join(digit, dim, own, came):
    rows, cols = own.shape
    whole = (rows, 2 * cols) if dim else (2 * rows, cols)
    steps = in_columns(whole, dim)
    of = lambda shape: pl.BlockSpec((shape[0], shape[1] // steps), lambda j: (0, j))
    return pl.pallas_call(
        functools.partial(join_kernel, dim),
        grid=(steps,),
        in_specs=[pl.BlockSpec(memory_space=SMEM), of((rows, cols)), of((rows, cols))],
        out_specs=of(whole),
        out_shape=result(whole, BF16, large(whole)),
        compiler_params=params(16),
        cost_estimate=cost(2 if large(whole) else 1),
        name="join",
    )(digit, *far((own, came), large((rows, cols))))


class Chain:
    def __init__(self, bits, plan, keep, send):
        self.bits, self.plan = bits, plan
        self.state = [keep, send]
        self.dims = [None]
        self.at = -1
        self.back = False
        self.done = False

    def work(self):
        bits, plan = self.bits, self.plan
        if not self.back:
            self.at += 1
            if self.at == 0:
                return
            if self.at == len(plan):
                self.at -= 1
                self.back = True
                (own,) = fold(bits.digit([plan[-1]]), 1, self.state)
                self.state = [own, own]
                return
            self.dims.append(cut(self.state[0].shape, 2))
            self.state = list(fold(bits.digit([plan[self.at]]), 2, self.state))
            return
        if self.at == 0:
            self.done = True
            return
        own = join(bits.digit([plan[self.at]]), self.dims[self.at], *self.state)
        self.at -= 1
        self.state = [own, own]

    def going(self):
        return self.state[:1] if self.back and not self.done else self.state

    def exchange(self):
        if not self.done:
            came = self.bits.send(self.state[1], [self.plan[self.at]], 1)
            self.state = [self.state[0], came]


def small_steps(bits):
    return [[b] for b in [bits.core, bits.across] + bits.seq]


def sum_small(bits, step, value):
    came = [bits.send(value, step, j) for j in range(1, 1 << len(step))]
    return functools.reduce(jnp.add, came, value)


def emit_feed_kernel(plan, count, me, digits, *refs):
    sources, (up, down, turned) = refs[: 2 * count], refs[-3:]
    size = plan.width // count
    own, other = sources[:count], sources[count:]
    for core, (ups, downs) in enumerate(((own, other), (other, own))):

        @pl.when(me[0] % 2 == core)
        def _(ups=ups, downs=downs):
            for j in range(count):
                rows = pl.ds(pl.multiple_of((digits[0] ^ j) * size, 16), size)
                up[rows, :] = ups[j][...].astype(F32)
                rows = pl.ds(pl.multiple_of((digits[1] ^ j) * size, 16), size)
                turned[rows, :] = downs[j][...]

    eye = jnp.where(
        lax.broadcasted_iota(jnp.int32, (plan.width, plan.width), 0)
        == lax.broadcasted_iota(jnp.int32, (plan.width, plan.width), 1),
        1.0,
        0.0,
    ).astype(BF16)
    down[...] = dot(turned[...], eye, TN)


def emit_feed(plan, me, digits, layer, layers, sources, before):
    cols = plan.hidden // FF_STEPS
    of = lambda a: pl.BlockSpec((a.shape[0], cols), lambda j: (0, j))
    anywhere = pl.BlockSpec(memory_space=pl.ANY)
    smem = pl.BlockSpec(memory_space=SMEM)

    def kernel(me_ref, digits_ref, *refs):
        ins, outs = refs[: len(sources)], refs[len(sources) + len(before) :]
        emit_feed_kernel(plan, len(sources) // 2, me_ref, digits_ref, *ins, *outs)

    return pl.pallas_call(
        kernel,
        grid=(FF_STEPS,),
        in_specs=[smem, smem] + [of(a) for a in sources] + [anywhere] * len(before),
        out_specs=[
            pl.BlockSpec((None, plan.width, cols), lambda j: (layer, 0, j)),
            pl.BlockSpec((None, cols, plan.width), lambda j: (layer, j, 0)),
        ],
        out_shape=[
            jax.ShapeDtypeStruct((layers, plan.width, plan.hidden), F32),
            jax.ShapeDtypeStruct((layers, plan.hidden, plan.width), F32),
        ],
        scratch_shapes=[pltpu.VMEM((plan.width, cols), BF16)],
        input_output_aliases={2 + len(sources) + i: i for i in range(len(before))},
        compiler_params=params(16),
        cost_estimate=cost(4),
        name="emit_feed",
    )(me, digits, *far(sources), *before)


def emit_heads_kernel(plan, layers, digit, *refs):
    sources, (into, out) = refs[:-2], refs[-2:]
    local = plan.local
    count = plan.width // len(sources)

    def put(ref, rows):
        for layer in range(layers):
            at = layer * 4 * local
            for t in range(3):
                into[layer, t, rows, :] = ref[:, at + t * local : at + (t + 1) * local].astype(F32)
            out[layer, :, rows] = ref[:, at + 3 * local : at + 4 * local].astype(F32).T

    if len(sources) == 1:
        put(sources[0], slice(0, count))
        return
    for mine in range(2):

        @pl.when(digit[0] == mine)
        def _(mine=mine):
            for j, ref in enumerate(sources):
                put(ref, slice((mine ^ j) * count, ((mine ^ j) + 1) * count))


def emit_heads(plan, digit, layers, sources):
    shapes = [(layers, 3, plan.width, plan.local), (layers, plan.local, plan.width)]
    return pl.pallas_call(
        functools.partial(emit_heads_kernel, plan, layers),
        grid=(1,),
        in_specs=[pl.BlockSpec(memory_space=SMEM)] + [full(a.shape) for a in sources],
        out_specs=[full(s) for s in shapes],
        out_shape=[jax.ShapeDtypeStruct(s, F32) for s in shapes],
        compiler_params=params(24),
        cost_estimate=cost(2),
        name="emit_heads",
    )(digit, *far(sources))


def body(
    tokens,
    actions,
    action_mask,
    frame_mask,
    environment_id,
    environment_embed,
    norm_gain,
    norm_bias,
    input_weight,
    output_weight,
    output_bias,
    up_weight,
    up_bias,
    down_weight,
    down_bias,
    cotangent,
):
    rows, width = tokens.shape
    seqs, frames, _ = actions.shape
    layers = input_weight.shape[0]
    envs = environment_embed.shape[0]
    plan = Plan(
        rows,
        lax.axis_size("head"),
        seqs,
        frames,
        width,
        input_weight.shape[3],
        up_weight.shape[2],
    )
    bits = Bits()
    me = lax.axis_index("head").astype(jnp.int32).reshape(1)
    as_rows = lambda t: t.reshape(layers, 1, -1)
    env_row = environment_id.reshape(1, seqs)
    stream, normed, *masks = prologue(
        plan,
        me,
        action_mask,
        frame_mask,
        env_row,
        tokens,
        actions,
        environment_embed,
        norm_gain,
        norm_bias,
    )
    own_slot, other_slots = [0], [1, 2]
    saved = []
    for layer in range(layers):
        away = False
        core, across = swap(normed, 1), swap(normed, 2)
        first = attend(plan, layer, own_slot, me, (normed, core), input_weight, masks, away)
        across, first = tie(across, first)
        blocks = (normed, core, across, swap(across, 1))
        *second, to_diagonal, to_core, to_across, mine = attend(
            plan,
            layer,
            other_slots,
            me,
            blocks,
            input_weight,
            masks,
            away,
            output_weight,
            first[1],
        )
        parts = scatter((to_diagonal, to_core, to_across, mine))
        middle, lifted, hidden, slope, *tail = forward_rest(
            plan,
            layer,
            layers,
            stream,
            parts,
            as_rows(output_bias),
            norm_gain,
            norm_bias,
            up_weight,
            as_rows(up_bias),
            down_weight,
            as_rows(down_bias),
        )
        saved.append((stream, blocks, first, second, middle, lifted, hidden, slope))
        if layer < layers - 1:
            stream, normed = tail
    mixed = tail[0]
    carry = jnp.pad(cotangent.astype(F32), ((0, plan.block - rows), (0, 0)))
    by_steps = len(bits.seq) == 3
    zero = jnp.zeros_like(me)
    stream, blocks, first, second, middle, lifted, hidden, slope = saved[-1]
    last = layers - 1

    def feed_back(layer, carry):
        stream, blocks, first, second, middle, lifted, hidden, slope = saved[layer]
        away = layer < last
        low, before_low, middle_grad, middle_low, second_sums, up_sums = back_rest(
            plan, layer, carry, middle, slope, norm_gain, up_weight, down_weight, away
        )
        core, across = swap(middle_low, 1), swap(middle_low, 2)
        by_chain = by_steps and layer == 0
        if layer == 0:
            own_grad = own_back(layer, middle_low, core)
            lifted, own_grad = tie(lifted, own_grad)
        else:
            lifted, core = tie(lifted, core)
            own_grad = None
        feed = feed_grads(
            plan, me if by_chain else zero, lifted, before_low, low, hidden, away
        )
        core, feed = tie(core, feed)
        return middle_grad, middle_low, core, across, own_grad, feed, second_sums, up_sums

    def own_back(layer, middle_low, core):
        return attend_back(
            plan,
            layer,
            [0],
            me,
            (middle_low, core),
            output_weight,
            masks,
            saved[layer][2],
            True,
        )[0]

    def start(chain, value):
        chain.state, value = tie(chain.state, value)
        chain.work()
        chain.state, value = tie(chain.state, value)
        chain.exchange()
        return value

    feed_plan = [bits.core] + bits.seq[:2] + [bits.across] + bits.seq[2:]
    held = {}

    def finish(state):
        middle_grad, middle_low, core, across, own_grad, last_sums = state
        heads, sums = {}, {}
        feed = None
        for layer in reversed(range(layers)):
            stream, blocks, first, second, middle, lifted, hidden, slope = saved[layer]
            tail = by_steps and layer == 0
            if layer < last:
                middle_grad, middle_low, core, across, own_grad, feed, *last_sums = feed_back(layer, carry)
                if tail:
                    feed = Chain(bits, feed_plan, *feed)
                    across = start(feed, across)
            else:
                across, own_grad = tie(across, own_grad)
            middle_blocks = (middle_low, core, across, swap(across, 1))
            if tail:
                middle_blocks = start(feed, middle_blocks)
            both_grad, *outs = attend_back(
                plan,
                layer,
                [1, 2],
                me,
                middle_blocks,
                output_weight,
                masks,
                second,
                True,
                input_weight,
                (own_grad,),
            )
            if tail:
                outs, feed.state = tie(outs, feed.state)
            to_diagonal, to_core, to_across, mine = outs
            from_diagonal = swap(to_diagonal, 1)
            from_core = swap(to_core, 1)
            pair = (to_across.astype(F32) + from_diagonal.astype(F32)).astype(BF16)
            pair_came = swap(pair, 2)
            if tail:
                feed.work()
                blocks, feed.state = tie(blocks, feed.state)
                feed.exchange()
            out_pair = (middle_blocks, (first[1], second[1]))
            parts = (mine, from_core, pair_came)
            if tail:
                parts, feed.state = tie(parts, feed.state)
            else:
                in_pair = (blocks, (own_grad, both_grad))
                (heads[layer],) = head_grads(plan, me, zero, 1, (in_pair, out_pair))
                parts, heads[layer] = tie(parts, heads[layer])
            carry, sums[layer] = carry_back(
                plan,
                layer,
                me,
                env_row,
                envs,
                parts,
                stream,
                middle_grad,
                norm_gain,
                [] if layer else [*last_sums] + [s for l in range(1, layers) for s in sums[l]],
                True,
            )
            if tail:
                sums[layer] = start(feed, sums[layer])
                blocks, sums[layer] = tie(blocks, sums[layer])
                in_pair = (blocks, (own_grad, both_grad))
                digit = bits.digit([bits.seq[0]])
                halves = head_grads(
                    plan, me, digit, 2, (in_pair, out_pair), [heads[l] for l in range(1, layers)]
                )
                halves, feed.state = tie(halves, feed.state)
                heads = Chain(bits, bits.seq, *halves)
            if layer:
                sums[layer] = (*last_sums, sums[layer])
        small = sums[0]
        if by_steps:
            for step in small_steps(bits)[:CUT]:
                small = start(feed, small)
                small = start(heads, small)
                small = sum_small(bits, step, small)
            for chain in (feed, heads):
                chain.state, small = tie(chain.state, small)
                chain.work()
            held["chains"] = [feed, heads]
            return carry, small, [feed.going(), heads.going()]
        small, feed = lax.psum((small, feed), ("seq", "head"))
        heads = lax.psum(jnp.concatenate([heads[l] for l in range(layers)], axis=1), "seq")
        return carry, small, [list(feed), [heads]]

    assert layers == 2
    middle_grad, middle_low, core, across, _, feed, *last_sums = feed_back(last, carry)
    feed_total = lax.psum(feed, ("seq", "head"))
    own_grad = own_back(last, middle_low, core)
    across, own_grad = tie(across, own_grad)
    state = (middle_grad, middle_low, core, across, own_grad, tuple(last_sums))
    shapes = jax.eval_shape(finish, state)
    carry, small, states = lax.cond(
        frame_mask[0, 0, 0] > 0,
        finish,
        lambda _: jax.tree.map(lambda s: jnp.zeros(s.shape, s.dtype), shapes),
        state,
    )
    states, small, feed_total = tie(states, small, feed_total)
    two = jnp.zeros((2,), jnp.int32)
    if by_steps:
        feed, heads = held["chains"]
        for chain, state in zip((feed, heads), states):
            chain.state = list(state) * (3 - len(state))
        rest = small_steps(bits)[CUT:]
        assert feed.at == 1
        mine = feed.state[0]
        came = bits.send(mine, [feed_plan[1]], 1)
        from_core = bits.send(mine, [bits.core], 1)
        heads.exchange()
        for step in rest:
            small = sum_small(bits, step, small)
        filled = emit_feed(plan, zero, two, last, layers, feed_total, ())
        came, filled, small = tie(came, filled, small)
        also_core = bits.send(came, [bits.core], 1)
        while not heads.done:
            heads.work()
            heads.exchange()
        digits = jnp.concatenate([bits.bit(mask) for mask in feed_plan[1]])
        sources = [mine, came, from_core, also_core]
        feed_out = emit_feed(plan, me, digits, 0, layers, sources, filled)
        digit = bits.digit([bits.seq[0]])
        heads, feed_out = tie(heads.state, feed_out)
    else:
        filled = emit_feed(plan, zero, two, last, layers, feed_total, ())
        feed, heads = states
        feed_out = emit_feed(plan, zero, two, 0, layers, feed, filled)
        digit = zero
    head_out = emit_heads(plan, digit, layers, heads)
    environment_total, gain_out, shift_out, out_bias_out, up_bias_out, down_bias_out = emit_small(
        plan, layers, envs, small
    )
    return (
        mixed,
        carry,
        environment_total,
        gain_out,
        shift_out,
        head_out[0],
        head_out[1],
        out_bias_out,
        feed_out[0],
        up_bias_out,
        feed_out[1],
        down_bias_out,
    )


def solution(mesh):
    return jax.shard_map(
        body,
        mesh=mesh,
        in_specs=(
            P(("seq", "head"), None),
            P("seq", None, None),
            P("seq", None),
            P("seq", None, None),
            P("seq"),
            P(),
            P(),
            P(),
            P(None, None, None, "head"),
            P(None, "head", None),
            P(),
            P(),
            P(),
            P(),
            P(),
            P(("seq", "head"), None),
        ),
        out_specs=(
            P(("seq", "head"), None),
            P(("seq", "head"), None),
            P(),
            P(),
            P(),
            P(None, None, None, "head"),
            P(None, "head", None),
            P(),
            P(),
            P(),
            P(),
            P(),
        ),
        check_vma=False,
    )
```

```python
import functools
import math

import jax
import jax.numpy as jnp
from jax import lax
from jax.experimental import pallas as pl
from jax.experimental.pallas import tpu as pltpu
from jax.sharding import PartitionSpec as P

HEAD_DIM = 64
EPSILON = 1e-05
MASKED = -1e30
LOG2E = math.log2(math.e)
LN2 = math.log(2.0)
LANES = 128
BF16 = jnp.bfloat16
F32 = jnp.float32
NT = (((1,), (1,)), ((), ()))
NN = (((1,), (0,)), ((), ()))
TN = (((0,), (0,)), ((), ()))
MIB = 1024 * 1024
SMEM = pltpu.MemorySpace.SMEM


def up_to(value, step):
    return -(-value // step) * step


def dot(a, b, dims=NN):
    return lax.dot_general(a, b, dims, preferred_element_type=F32)


class Plan:
    def __init__(self, rows, groups, seqs, frames, width, local_width, hidden):
        self.rows, self.groups, self.seqs, self.frames = rows, groups, seqs, frames
        self.width, self.local, self.hidden = width, local_width, hidden
        self.block = up_to(rows, 16)
        self.total = self.block * groups
        self.length = rows * groups // seqs
        self.patches = self.length // frames
        self.heads = local_width // HEAD_DIM
        self.group_lanes = LANES // self.heads
        place = lambda t: t // rows * self.block + t % rows
        starts = [place(s * self.length) // 16 * 16 for s in range(seqs)]
        ends = [place((s + 1) * self.length - 1) + 1 for s in range(seqs)]
        self.window = max(up_to(e - s, 16) for s, e in zip(starts, ends))
        self.stride = starts[1] - starts[0]
        assert seqs == 3 and groups == 4
        assert starts == [self.stride * s for s in range(seqs)]
        assert self.window <= 2 * self.block
        assert starts[-1] + self.window <= self.total
        self.lanes = up_to(self.window, LANES)
        first = [
            min(place(s * self.length + f * self.patches) - starts[s] for s in range(seqs))
            for f in range(frames)
        ]
        last = [
            max(
                place(s * self.length + (f + 1) * self.patches - 1) - starts[s] + 1
                for s in range(seqs)
            )
            for f in range(frames)
        ]
        self.cuts = [first[f] // 16 * 16 if f else 0 for f in range(frames)] + [self.window]
        ends = [0] + [min(up_to(last[f], LANES), self.lanes) for f in range(frames - 1)] + [self.lanes]
        self.key_chunks = [
            (ends[f], ends[f + 1] - ends[f], self.cuts[f]) for f in range(frames)
        ]
        begins = [first[f] // LANES * LANES if f else 0 for f in range(frames)] + [self.lanes]
        reach = [up_to(last[f], 16) for f in range(frames - 1)] + [self.window]
        self.query_chunks = [
            (begins[f], begins[f + 1] - begins[f], reach[f]) for f in range(frames)
        ]

    def sequence(self, slot, across):
        if slot == 2:
            return 1
        return across * (self.seqs - 1) if slot == 0 else (1 - across) * (self.seqs - 1)


def params(mib):
    return pltpu.CompilerParams(vmem_limit_bytes=mib * MIB)


def result(shape, dtype, away=False):
    return pltpu.HBM(shape, dtype) if away else jax.ShapeDtypeStruct(shape, dtype)


def far(arrays, away=True):
    return [pltpu.with_memory_space_constraint(a, pltpu.HBM) if away else a for a in arrays]


def cost(microseconds):
    return pl.CostEstimate(flops=0, bytes_accessed=int(3.69e6 * microseconds), transcendentals=0)


def full(shape):
    return pl.BlockSpec(shape, lambda *i: (0,) * len(shape))


def layer_of(shape, layer):
    return pl.BlockSpec((None,) + shape, lambda *i: (layer,) + (0,) * len(shape))


def norm_stats(values):
    center = values - jnp.mean(values, axis=-1, keepdims=True)
    spread = jnp.mean(center * center, axis=-1, keepdims=True)
    return center, lax.rsqrt(spread + EPSILON)


def norm_back(upstream, center, scale, gain):
    unit = center * scale
    weighted = upstream * gain
    mean_w = jnp.mean(weighted, axis=-1, keepdims=True)
    mean_wn = jnp.mean(weighted * unit, axis=-1, keepdims=True)
    grad = scale * (weighted - mean_w - unit * mean_wn)
    return (
        grad,
        jnp.sum(upstream * unit, axis=0, keepdims=True),
        jnp.sum(upstream, axis=0, keepdims=True),
    )


def prologue_kernel(
    plan, me_ref, act_mask, frame_mask, env_id, tokens, actions, embed, gain, shift, stream, normed, qhot, kbias, valid
):
    rows, block = plan.rows, plan.block
    row = lax.broadcasted_iota(jnp.int32, (block, plan.width), 0)
    place = me_ref[0] * rows + row
    condition = jnp.zeros((block, plan.width), F32)
    for s in range(plan.seqs):
        env = jnp.zeros((1, plan.width), F32)
        for e in range(embed.shape[0]):
            env = jnp.where(env_id[0:1, s : s + 1] == e, embed[e : e + 1, :], env)
        for f in range(plan.frames):
            mask = act_mask[s : s + 1, f : f + 1].astype(F32)
            term = actions[s, f : f + 1, :].astype(F32) * mask + env
            begin = s * plan.length + f * plan.patches
            condition = jnp.where(
                (place >= begin) & (place < begin + plan.patches), term, condition
            )
    padded = jnp.concatenate(
        [tokens[...].astype(F32), jnp.zeros((block - rows, plan.width), F32)], axis=0
    )
    values = jnp.where(row < rows, padded + condition, 0.0)
    stream[...] = values
    center, scale = norm_stats(values)
    normed[...] = (center * scale * gain[0:1, :] + shift[0:1, :]).astype(BF16)
    line = lax.broadcasted_iota(jnp.int32, (plan.lanes, LANES), 0)
    lane = lax.broadcasted_iota(jnp.int32, (plan.lanes, LANES), 1) % plan.group_lanes
    for slot in range(plan.seqs):
        s = plan.sequence(slot, me_ref[0] // 2)
        at = plan.stride * s + line
        origin = at
        inside = line < plan.window
        for b in range(plan.groups):
            here = (at >= b * block) & (at < (b + 1) * block)
            origin = jnp.where(here, at - b * (block - rows), origin)
            inside = inside & jnp.logical_not(here & (at >= b * block + rows))
        token = origin - s * plan.length
        inside = inside & (token >= 0) & (token < plan.length)
        frame = jnp.zeros_like(token)
        for f in range(1, plan.frames):
            frame = frame + jnp.where(token >= f * plan.patches, 1, 0)
        frame = jnp.where(inside, frame, -1)
        qhot[slot] = jnp.where((lane == frame) & inside, 1.0, 0.0).astype(BF16)
        valid[slot] = jnp.where(inside, 1.0, 0.0)[: plan.window].astype(BF16)
        bias = jnp.where(lane < plan.frames, MASKED, 0.0)
        bias = jnp.where((lane >= plan.frames) & (lane < plan.frames + 3), 1.0, bias)
        allowed = frame_mask[s]
        for f in range(plan.frames):
            for g in range(plan.frames):
                value = jnp.where(allowed[f : f + 1, g : g + 1] > 0, 0.0, MASKED)
                bias = jnp.where((lane == f) & (frame == g), value, bias)
        kbias[slot] = bias.astype(BF16)


def prologue(plan, me, action_mask, frame_mask, env_id, tokens, actions, embed, gain, shift):
    return pl.pallas_call(
        functools.partial(prologue_kernel, plan),
        grid=(1,),
        in_specs=[pl.BlockSpec(memory_space=SMEM)]
        + [full(action_mask.shape), full(frame_mask.shape), full(env_id.shape)]
        + [full(tokens.shape), full(actions.shape), full(embed.shape)]
        + [layer_of(gain.shape[1:], 0), layer_of(gain.shape[1:], 0)],
        out_specs=[
            full((plan.block, plan.width)),
            full((plan.block, plan.width)),
            full((plan.seqs, plan.lanes, LANES)),
            full((plan.seqs, plan.lanes, LANES)),
            full((plan.seqs, plan.window, LANES)),
        ],
        out_shape=[
            jax.ShapeDtypeStruct((plan.block, plan.width), F32),
            jax.ShapeDtypeStruct((plan.block, plan.width), BF16),
            result((plan.seqs, plan.lanes, LANES), BF16),
            result((plan.seqs, plan.lanes, LANES), BF16),
            result((plan.seqs, plan.window, LANES), BF16),
        ],
        compiler_params=params(16),
        cost_estimate=cost(5),
        name="prologue",
    )(me, *far([action_mask, frame_mask, env_id, tokens, actions, embed, gain, shift]))


def place_blocks(plan, me, blocks, target):
    x, c = me[0] // 2, me[0] % 2
    if len(blocks) == 2:
        order = [c, 1 - c]
    else:
        order = [2 * x + c, 2 * x + 1 - c, 2 * (1 - x) + c, 2 * (1 - x) + 1 - c]
    for ref, b in zip(blocks, order):
        target[pl.ds(pl.multiple_of(b * plan.block, 16), plan.block), :] = ref[...]


def scatter_blocks(plan, me, block_of, outs):
    x, c = me[0] // 2, me[0] % 2
    order = [2 * (1 - x) + 1 - c, 2 * x + 1 - c, 2 * (1 - x) + c, 2 * x + c]
    for ref, b in zip(outs, order):
        rows = pl.ds(pl.multiple_of(b * plan.block, 16), plan.block)
        ref[...] = block_of(rows).astype(BF16)


def window_start(plan, me, slots, blocks):
    x = me[0] // 2
    if len(slots) == 1:
        s = plan.sequence(slots[0], x)
    else:
        s = jnp.int32(0)
        for i, slot in enumerate(slots):
            s = jnp.where(pl.program_id(0) == i, plan.sequence(slot, x), s)
    start = s * plan.stride
    if blocks == 2:
        start = start - x * (2 * plan.block)
    return pl.multiple_of(start, 16)


def group_mask(plan, head):
    lane = lax.broadcasted_iota(jnp.int32, (1, LANES), 1)
    return jnp.where(lane // plan.group_lanes == head, 1.0, 0.0).astype(BF16)


def put_windows(plan, me, slots, before, target, value):
    over = plan.window - plan.stride
    step = pl.program_id(0)
    at = window_start(plan, me, slots, 4)

    @pl.when(step == 0)
    def _():
        target[...] = jnp.zeros(target.shape, target.dtype)
        for slot, ref in enumerate(before):
            start = pl.multiple_of(plan.sequence(slot, me[0] // 2) * plan.stride, 16)
            target[pl.ds(start, plan.window), :] = ref[0]

    inner = pl.ds(pl.multiple_of(at + over, 16), plan.window - 2 * over)
    target[inner, :] = value[over : plan.window - over]
    for begin in (0, plan.window - over):
        rows = pl.ds(pl.multiple_of(at + begin, 16), over)
        target[rows, :] = target[rows, :] + value[begin : begin + over]


def attend_kernel(plan, slots, blocks, *refs):
    me, refs = refs[0], refs[1:]
    placed, refs = refs[:blocks], refs[blocks:]
    w_in, qhot, kbias, valid = refs[:4]
    refs = refs[4:]
    last = blocks == 4
    if last:
        w_out, before, refs = refs[0], refs[1], refs[2:]
    triple, attention, lse = refs[:3]
    refs = refs[3:]
    if last:
        outs, refs = refs[:4], refs[4:]
    gathered, q_even, q_odd, keys, values, *whole = refs
    window, local = plan.window, plan.local

    @pl.when(pl.program_id(0) == 0)
    def _():
        place_blocks(plan, me, placed, gathered)
        keys[window:, :] = jnp.zeros((plan.lanes - window, local), BF16)
        values[window:, :] = jnp.zeros((plan.lanes - window, local), BF16)

    x = gathered[pl.ds(window_start(plan, me, slots, blocks), window), :]
    query = dot(x, w_in[0]) * (HEAD_DIM ** (-0.5) * LOG2E)
    odd_lane = lax.broadcasted_iota(jnp.int32, (1, local), 1) // HEAD_DIM % 2 == 1
    q_even[...] = jnp.where(odd_lane, 0.0, query).astype(BF16)
    q_odd[...] = jnp.where(odd_lane, query, 0.0).astype(BF16)
    triple[0, :, 0:local] = query.astype(BF16)
    key = dot(x, w_in[1]).astype(BF16)
    triple[0, :, local : 2 * local] = key
    keys[0:window, :] = key
    value = dot(x, w_in[2]).astype(BF16)
    triple[0, :, 2 * local : 3 * local] = value
    values[0:window, :] = value
    left = lax.broadcasted_iota(jnp.int32, (1, LANES), 1) < HEAD_DIM
    lane_head = lax.broadcasted_iota(jnp.int32, (1, LANES), 1) // plan.group_lanes
    chunks = plan.key_chunks
    spans = list(zip(plan.cuts[:-1], plan.cuts[1:]))

    def scores_of(head):
        cols = slice(head // 2 * LANES, (head // 2 + 1) * LANES)
        q = (q_even, q_odd)[head % 2]
        pick = group_mask(plan, head)
        scores = []
        for k0, count, r0 in chunks:
            lhs = jnp.concatenate([q[r0:, cols], qhot[0, r0:window, :]], axis=1)
            rhs = jnp.concatenate(
                [keys[k0 : k0 + count, cols], kbias[0, k0 : k0 + count, :] * pick], axis=1
            )
            scores.append(dot(lhs, rhs, NT))
        return scores

    def soften(scores):
        tops, weights = [], [[] for _ in chunks]
        for i, (begin, end) in enumerate(spans):
            pieces = [scores[c][begin - chunks[c][2] : end - chunks[c][2]] for c in range(i + 1)]
            top = jnp.max(jnp.concatenate(pieces, axis=1), axis=-1, keepdims=True)
            tops.append(jnp.broadcast_to(top, (end - begin, LANES)))
            for c in range(i + 1):
                weights[c].append(jnp.exp2(pieces[c] - top).astype(BF16))
        return jnp.concatenate(tops, axis=0), [jnp.concatenate(w, axis=0) for w in weights]

    def mix(head, weights):
        cols = slice(head // 2 * LANES, (head // 2 + 1) * LANES)
        parts = []
        for (k0, count, _), weight in zip(chunks, weights):
            rhs = jnp.concatenate(
                [values[k0 : k0 + count, cols], jnp.ones((count, LANES), BF16)], axis=1
            )
            parts.append(dot(weight, rhs))
        rows = []
        for i, (begin, end) in enumerate(spans):
            pieces = [parts[c][begin - chunks[c][2] : end - chunks[c][2]] for c in range(i + 1)]
            rows.append(functools.reduce(jnp.add, pieces))
        return jnp.concatenate(rows, axis=0)

    state = {}

    def finish(head, top, mixed):
        total = mixed[:, LANES:]
        state[head] = mixed[:, :LANES] / total
        if head == 0:
            state["top"], state["total"] = top, total
        else:
            state["top"] = jnp.where(lane_head == head, top, state["top"])
            state["total"] = jnp.where(lane_head == head, total, state["total"])
        if head % 2 == 1:
            both = jnp.where(left, state[head - 1], state[head]) * valid[0].astype(F32)
            attention[0, :, (head // 2) * LANES : (head // 2 + 1) * LANES] = both.astype(BF16)

    heads = plan.heads
    scores = {h: scores_of(h) for h in range(min(2, heads))}
    soft, mixed = {}, {}
    for h in range(heads):
        soft[h] = soften(scores.pop(h))
        if h + 2 < heads:
            scores[h + 2] = scores_of(h + 2)
        mixed[h] = mix(h, soft[h][1])
        if h >= 1:
            finish(h - 1, soft[h - 1][0], mixed.pop(h - 1))
    finish(heads - 1, soft[heads - 1][0], mixed.pop(heads - 1))
    lse[0] = state["top"] + jnp.log2(state["total"])
    if last:
        put_windows(plan, me, slots, [before], whole[0], attention[0])

        @pl.when(pl.program_id(0) == len(slots) - 1)
        def _():
            scatter_blocks(plan, me, lambda rows: dot(whole[0][rows, :], w_out[...]), outs)


def per_slot(slots, shape):
    first = slots[0]
    return pl.BlockSpec((1,) + shape, lambda s: (s + first,) + (0,) * len(shape))


def attend(plan, layer, slots, me, blocks, input_weight, masks, away, output_weight=None, before=None):
    block = (plan.block, plan.width)
    n = len(slots)
    last = before is not None
    each = lambda shape: pl.BlockSpec((1,) + shape, lambda s: (s, 0, 0))
    shape = lambda *dims: result((n, plan.window) + dims, BF16, away)
    in_specs = [pl.BlockSpec(memory_space=SMEM)] + [full(block)] * len(blocks)
    in_specs += [layer_of(input_weight.shape[1:], layer)]
    in_specs += [per_slot(slots, m.shape[1:]) for m in masks]
    out_specs = [
        each((plan.window, 3 * plan.local)),
        each((plan.window, plan.local)),
        each((plan.window, LANES)),
    ]
    out_shape = [
        shape(3 * plan.local),
        shape(plan.local),
        result((n, plan.window, LANES), F32, away),
    ]
    scratch = [
        pltpu.VMEM((len(blocks) * plan.block, plan.width), BF16),
        pltpu.VMEM((plan.window, plan.local), BF16),
        pltpu.VMEM((plan.window, plan.local), BF16),
        pltpu.VMEM((plan.lanes, plan.local), BF16),
        pltpu.VMEM((plan.lanes, plan.local), BF16),
    ]
    args = [me, *blocks, input_weight, *masks]
    if last:
        in_specs += [layer_of(output_weight.shape[1:], layer), full(before.shape)]
        args += [output_weight, before]
        out_specs += [full(block)] * 4
        out_shape += [jax.ShapeDtypeStruct(block, BF16)] * 4
        scratch += [pltpu.VMEM((plan.total, plan.local), BF16)]
    area = plan.window * plan.lanes * plan.heads
    return pl.pallas_call(
        functools.partial(attend_kernel, plan, slots, len(blocks)),
        grid=(n,),
        in_specs=in_specs,
        out_specs=out_specs,
        out_shape=out_shape,
        scratch_shapes=scratch,
        compiler_params=params(20),
        cost_estimate=cost(3 * n),
        name="attend",
    )(*args)


def three_parts(value):
    high = value.astype(BF16)
    rest = value - high.astype(F32)
    middle = rest.astype(BF16)
    low = (rest - middle.astype(F32)).astype(BF16)
    return high.astype(F32), middle.astype(F32), low.astype(F32)


def attend_back_kernel(plan, slots, blocks, *refs):
    me, refs = refs[0], refs[1:]
    placed, refs = refs[:blocks], refs[blocks:]
    w_out, qhot, kbias, valid, triple, attention, lse = refs[:7]
    refs = refs[7:]
    last = slots[-1] == plan.seqs - 1
    if last:
        w_in, before, refs = refs[0], refs[1 : 1 + slots[0]], refs[1 + slots[0] :]
    triple_grad, refs = refs[0], refs[1:]
    if last:
        outs, refs = refs[:4], refs[4:]
    gathered, queries, grads, query_side, grad_side, key_turned, *whole = refs
    window, local, lanes = plan.window, plan.local, plan.lanes

    @pl.when(pl.program_id(0) == 0)
    def _():
        place_blocks(plan, me, placed, gathered)
        queries[window:, :] = jnp.zeros((lanes - window, local), BF16)
        grads[window:, :] = jnp.zeros((lanes - window, local), BF16)
        query_side[window:, :] = jnp.zeros((lanes - window, LANES), BF16)
        grad_side[window:, :] = jnp.zeros((lanes - window, LANES), BF16)

    mask = valid[0].astype(F32)
    head_grad = dot(gathered[pl.ds(window_start(plan, me, slots, blocks), window), :], w_out[...], NT)
    head_grad = head_grad * jnp.concatenate([mask] * (local // LANES), axis=1)
    head_grad = head_grad.astype(BF16)
    grads[0:window, :] = head_grad
    queries[0:window, :] = triple[0, :, 0:local]
    key_turned[...] = triple[0, :, local : 2 * local].T
    product = head_grad.astype(F32) * attention[0].astype(F32)
    high = product.astype(BF16)
    low = (product - high.astype(F32)).astype(BF16)
    spread = jnp.where(
        lax.broadcasted_iota(jnp.int32, (local, LANES), 0) // HEAD_DIM
        == lax.broadcasted_iota(jnp.int32, (local, LANES), 1) // plan.group_lanes,
        1.0,
        0.0,
    ).astype(BF16)
    inner = dot(high, spread) + dot(low, spread)
    slot = lax.broadcasted_iota(jnp.int32, (1, LANES), 1) % plan.group_lanes
    a, b, c = three_parts(-inner)
    grad_side[0:window, :] = jnp.where(
        slot == 0, a, jnp.where(slot == 1, b, jnp.where(slot == 2, c, 0.0))
    ).astype(BF16)
    a, b, c = three_parts(-lse[0])
    n = plan.frames
    query_side[0:window, :] = jnp.where(
        slot < n,
        qhot[0, 0:window, :].astype(F32),
        jnp.where(slot == n, a, jnp.where(slot == n + 1, b, jnp.where(slot == n + 2, c, 0.0))),
    ).astype(BF16)
    left = lax.broadcasted_iota(jnp.int32, (1, LANES), 1) < HEAD_DIM
    sides = [jnp.where(left, 1.0, 0.0).astype(BF16), jnp.where(left, 0.0, 1.0).astype(BF16)]
    chunks = plan.query_chunks
    ends = [0] + [c[2] for c in chunks]

    def products(head):
        half = head % 2
        tile = head // 2 * LANES
        cols = slice(tile, tile + LANES)
        pick = group_mask(plan, head)
        ones = jnp.where(slot < 3, pick.astype(F32), 0.0).astype(BF16)
        key_side = jnp.concatenate(
            [
                triple[0, :, local + tile : local + tile + LANES] * sides[half],
                kbias[0, 0:window, :] * pick,
            ],
            axis=1,
        )
        value_side = jnp.concatenate(
            [
                triple[0, :, 2 * local + tile : 2 * local + tile + LANES] * sides[half],
                jnp.broadcast_to(ones, (window, LANES)),
            ],
            axis=1,
        )
        scores, prob_grads = [], []
        for q0, count, reach in chunks:
            rows = slice(q0, q0 + count)
            rhs = jnp.concatenate([queries[rows, cols], query_side[rows, :]], axis=1)
            scores.append(dot(key_side[:reach], rhs, NT))
        for q0, count, reach in chunks:
            rows = slice(q0, q0 + count)
            rhs = jnp.concatenate([grads[rows, cols], grad_side[rows, :]], axis=1)
            prob_grads.append(dot(value_side[:reach], rhs, NT))
        return scores, prob_grads

    def pointwise(scores, prob_grads):
        probs = [jnp.exp2(s) for s in scores]
        score_grads = [(p * g).astype(BF16) for p, g in zip(probs, prob_grads)]
        return [p.astype(BF16) for p in probs], score_grads

    def add_rows(parts):
        rows = []
        for i in range(len(chunks)):
            pieces = [p[ends[i] : ends[i + 1]] for p in parts[i:]]
            rows.append(functools.reduce(jnp.add, pieces))
        return jnp.concatenate(rows, axis=0)

    def gradients(head, probs, score_grads):
        tile = head // 2 * LANES
        cols = slice(tile, tile + LANES)
        value_parts, key_parts, query_parts = [], [], []
        turned = key_turned[tile + head % 2 * HEAD_DIM : tile + (head % 2 + 1) * HEAD_DIM, :]
        for (q0, count, reach), prob in zip(chunks, probs):
            value_parts.append(dot(prob, grads[q0 : q0 + count, cols]))
        for (q0, count, reach), score_grad in zip(chunks, score_grads):
            key_parts.append(dot(score_grad, queries[q0 : q0 + count, cols]))
        for (q0, count, reach), score_grad in zip(chunks, score_grads):
            query_parts.append(dot(turned[:, :reach], score_grad))
        return jnp.concatenate(query_parts, axis=1), add_rows(key_parts), add_rows(value_parts)

    heads = plan.heads
    found = [products(h) for h in range(heads)]
    pointed = [pointwise(*f) for f in found]
    for tile in range(heads // 2):
        even, odd = (gradients(h, *pointed[h]) for h in (2 * tile, 2 * tile + 1))
        query = jnp.concatenate([even[0], odd[0]], axis=0).T[:window] * HEAD_DIM ** (-0.5)
        key = jnp.where(left, even[1], odd[1]) * LN2
        value = jnp.where(left, even[2], odd[2])
        for t, grad in enumerate((query, key, value)):
            at = t * local + tile * LANES
            triple_grad[0, :, at : at + LANES] = grad.astype(BF16)
    if last:
        put_windows(plan, me, slots, before, whole[0], triple_grad[0])

        @pl.when(pl.program_id(0) == len(slots) - 1)
        def _():
            def back(rows):
                total = dot(whole[0][rows, 0:local], w_in[0], NT)
                for t in (1, 2):
                    total = total + dot(whole[0][rows, t * local : (t + 1) * local], w_in[t], NT)
                return total

            scatter_blocks(plan, me, back, outs)


def attend_back(plan, layer, slots, me, blocks, output_weight, masks, saved, away, input_weight=None, before=None):
    block = (plan.block, plan.width)
    n = len(slots)
    last = before is not None
    each = lambda shape: pl.BlockSpec((1,) + shape, lambda s: (s, 0, 0))
    in_specs = [pl.BlockSpec(memory_space=SMEM)] + [full(block)] * len(blocks)
    in_specs += [layer_of(output_weight.shape[1:], layer)]
    in_specs += [per_slot(slots, m.shape[1:]) for m in masks]
    in_specs += [per_slot([max(slots[0] - 1, 0)], a.shape[1:]) for a in saved]
    out_specs = [each((plan.window, 3 * plan.local))]
    out_shape = [jax.ShapeDtypeStruct((n, plan.window, 3 * plan.local), BF16)]
    scratch = [
        pltpu.VMEM((len(blocks) * plan.block, plan.width), BF16),
        pltpu.VMEM((plan.lanes, plan.local), BF16),
        pltpu.VMEM((plan.lanes, plan.local), BF16),
        pltpu.VMEM((plan.lanes, LANES), BF16),
        pltpu.VMEM((plan.lanes, LANES), BF16),
        pltpu.VMEM((plan.local, plan.window), BF16),
    ]
    args = [me, *blocks, *far([output_weight, *masks, *saved])]
    if last:
        in_specs += [layer_of(input_weight.shape[1:], layer)] + [full(w.shape) for w in before]
        args += [*far([input_weight]), *before]
        out_specs += [full(block)] * 4
        out_shape += [jax.ShapeDtypeStruct(block, BF16)] * 4
        scratch += [pltpu.VMEM((plan.total, 3 * plan.local), BF16)]
    area = plan.window * plan.lanes * plan.heads
    return pl.pallas_call(
        functools.partial(attend_back_kernel, plan, slots, len(blocks)),
        grid=(n,),
        in_specs=in_specs,
        out_specs=out_specs,
        out_shape=out_shape,
        scratch_shapes=scratch,
        compiler_params=params(28),
        cost_estimate=cost(6 * n),
        name="attend_back",
    )(*args)


FF_STEPS = 2


def forward_kernel(plan, last, stream, part_a, part_b, part_c, out_bias, gain, shift, up, up_bias, down, down_bias, next_gain, next_shift, middle, lifted, hidden, slope, *rest):
    outs, total = rest[:-1], rest[-1]
    step = pl.program_id(0)

    @pl.when(step == 0)
    def _():
        projected = part_a[...].astype(F32) + part_b[...].astype(F32) + part_c[...].astype(F32)
        values = stream[...] + (projected + out_bias[...])
        middle[...] = values
        center, scale = norm_stats(values)
        lifted[...] = (center * scale * gain[1:2, :] + shift[1:2, :]).astype(BF16)
        total[...] = values + down_bias[...]

    before = dot(lifted[...], up[...]) + up_bias[...]
    cdf = 0.5 + 0.5 * lax.erf(before * (2.0**-0.5))
    density = jnp.exp2(before * before * (-0.5 * LOG2E)) * (2.0 * math.pi) ** -0.5
    act = (before * cdf).astype(BF16)
    hidden[...] = act
    slope[...] = (cdf + before * density).astype(BF16)
    total[...] += dot(act, down[...])

    @pl.when(step == FF_STEPS - 1)
    def _():
        values = total[...]
        if last:
            outs[0][...] = values.astype(BF16)[: plan.rows]
        else:
            outs[0][...] = values
            center, scale = norm_stats(values)
            outs[1][...] = (center * scale * next_gain[0:1, :] + next_shift[0:1, :]).astype(BF16)


def forward_rest(plan, layer, layers, stream, parts, output_bias, gain, shift, up, up_bias, down, down_bias):
    last = layer == layers - 1
    block = (plan.block, plan.width)
    cols = plan.hidden // FF_STEPS
    follow = min(layer + 1, layers - 1)
    wide = pl.BlockSpec((plan.block, cols), lambda j: (0, j))
    row = lambda width: layer_of((1, width), layer)
    if last:
        tail_specs = [full((plan.rows, plan.width))]
        tail = [jax.ShapeDtypeStruct((plan.rows, plan.width), BF16)]
    else:
        tail_specs = [full(block), full(block)]
        tail = [jax.ShapeDtypeStruct(block, F32), jax.ShapeDtypeStruct(block, BF16)]
    return pl.pallas_call(
        functools.partial(forward_kernel, plan, last),
        grid=(FF_STEPS,),
        in_specs=[full(block)] * 4
        + [
            row(plan.width),
            layer_of(gain.shape[1:], layer),
            layer_of(gain.shape[1:], layer),
            pl.BlockSpec((None, plan.width, cols), lambda j: (layer, 0, j)),
            pl.BlockSpec((None, 1, cols), lambda j: (layer, 0, j)),
            pl.BlockSpec((None, cols, plan.width), lambda j: (layer, j, 0)),
            row(plan.width),
            layer_of(gain.shape[1:], follow),
            layer_of(gain.shape[1:], follow),
        ],
        out_specs=[full(block), full(block), wide, wide] + tail_specs,
        out_shape=[
            result(block, F32),
            result(block, BF16),
            result((plan.block, plan.hidden), BF16),
            result((plan.block, plan.hidden), BF16),
        ]
        + tail,
        scratch_shapes=[pltpu.VMEM(block, F32)],
        compiler_params=params(20),
        cost_estimate=cost(5),
        name="forward_rest",
    )(stream, *parts, *far([output_bias, gain, shift]), up, *far([up_bias]), down, *far([down_bias, gain, shift]))


def back_kernel(plan, carry, middle, slope, gain, up, down, low, before_low, middle_grad, middle_low, sums, up_bias, total):
    step = pl.program_id(0)

    @pl.when(step == 0)
    def _():
        low[...] = carry[...].astype(BF16)
        total[...] = jnp.zeros(total.shape, F32)

    before_grad = dot(low[...], down[...], NT) * slope[...].astype(F32)
    up_bias[...] = jnp.sum(before_grad, axis=0, keepdims=True)
    narrow = before_grad.astype(BF16)
    before_low[...] = narrow
    total[...] += dot(narrow, up[...], NT)

    @pl.when(step == FF_STEPS - 1)
    def _():
        center, scale = norm_stats(middle[...])
        grad, gain_sum, shift_sum = norm_back(total[...], center, scale, gain[1:2, :])
        carried = carry[...]
        grad = carried + grad
        middle_grad[...] = grad
        middle_low[...] = grad.astype(BF16)
        sums[...] = jnp.zeros(sums.shape, F32)
        sums[0:1, :] = gain_sum
        sums[1:2, :] = shift_sum
        sums[2:3, :] = jnp.sum(grad, axis=0, keepdims=True)
        sums[3:4, :] = jnp.sum(carried, axis=0, keepdims=True)


def back_rest(plan, layer, carry, middle, slope, gain, up, down, away):
    block = (plan.block, plan.width)
    cols = plan.hidden // FF_STEPS
    wide = pl.BlockSpec((plan.block, cols), lambda j: (0, j))
    return pl.pallas_call(
        functools.partial(back_kernel, plan),
        grid=(FF_STEPS,),
        in_specs=[
            full(block),
            full(block),
            wide,
            layer_of(gain.shape[1:], layer),
            pl.BlockSpec((None, plan.width, cols), lambda j: (layer, 0, j)),
            pl.BlockSpec((None, cols, plan.width), lambda j: (layer, j, 0)),
        ],
        out_specs=[
            full(block),
            wide,
            full(block),
            full(block),
            full((8, plan.width)),
            pl.BlockSpec((1, cols), lambda j: (0, j)),
        ],
        out_shape=[
            jax.ShapeDtypeStruct(block, BF16),
            jax.ShapeDtypeStruct((plan.block, plan.hidden), BF16),
            jax.ShapeDtypeStruct(block, F32),
            jax.ShapeDtypeStruct(block, BF16),
            jax.ShapeDtypeStruct((8, plan.width), F32),
            jax.ShapeDtypeStruct((1, plan.hidden), F32),
        ],
        scratch_shapes=[pltpu.VMEM(block, F32)],
        compiler_params=params(20),
        cost_estimate=cost(6),
        name="back_rest",
    )(carry, *far((middle, slope), away), *far((gain, up, down)))


SMALL_ROWS = 8
CUT = 4


def carry_kernel(plan, wide, me, env_id, part_a, part_b, part_c, stream, middle_grad, gain, *rest):
    others, outs = rest[: len(rest) - 2], rest[-2:]
    carry, sums = outs
    upstream = part_a[...].astype(F32) + part_b[...].astype(F32) + part_c[...].astype(F32)
    center, scale = norm_stats(stream[...])
    grad, gain_sum, shift_sum = norm_back(upstream, center, scale, gain[0:1, :])
    grad = middle_grad[...] + grad
    carry[...] = grad[: carry.shape[0]]
    sums[...] = jnp.zeros(sums.shape, F32)
    sums[0:1, :] = gain_sum
    sums[1:2, :] = shift_sum
    if not others:
        return
    row = lax.broadcasted_iota(jnp.int32, (plan.block, plan.width), 0)
    place = me[0] * plan.rows + row
    envs = sums.shape[0] - SMALL_ROWS * (1 + len(others))
    line = lax.broadcasted_iota(jnp.int32, (envs, plan.width), 0)
    total = jnp.zeros((envs, plan.width), F32)
    for s in range(plan.seqs):
        inside = (row < plan.rows) & (place >= s * plan.length)
        inside = inside & (place < (s + 1) * plan.length)
        part = jnp.sum(jnp.where(inside, grad, 0.0), axis=0, keepdims=True)
        total = total + jnp.where(line == env_id[0:1, s : s + 1], part, 0.0)
    at = SMALL_ROWS
    for ref in others:
        if ref.shape[0] == 1:
            for i in range(SMALL_ROWS):
                sums[at + i : at + i + 1, 0:wide] = ref[:, i * wide : (i + 1) * wide]
        else:
            sums[at : at + SMALL_ROWS, :] = ref[...]
        at += SMALL_ROWS
    sums[at : at + envs, :] = total


def carry_back(plan, layer, me, env_id, envs, parts, stream, middle_grad, gain, others, away):
    block = (plan.block, plan.width)
    first = layer == 0
    rows = plan.rows if first else plan.block
    wide = plan.hidden // SMALL_ROWS
    assert wide <= plan.width and wide % LANES == 0
    small = SMALL_ROWS * (1 + len(others)) + (envs if first else 0)
    return pl.pallas_call(
        functools.partial(carry_kernel, plan, wide),
        grid=(1,),
        in_specs=[pl.BlockSpec(memory_space=SMEM), full(env_id.shape)]
        + [full(block)] * 5
        + [layer_of(gain.shape[1:], layer)]
        + [full(o.shape) for o in others],
        out_specs=[full((rows, plan.width)), full((small, plan.width))],
        out_shape=[
            jax.ShapeDtypeStruct((rows, plan.width), F32),
            jax.ShapeDtypeStruct((small, plan.width), F32),
        ],
        compiler_params=params(16),
        cost_estimate=cost(2),
        name="carry_back",
    )(me, *far([env_id]), *parts, *far([stream], away), middle_grad, *far([gain, *others]))


def emit_small_kernel(plan, layers, envs, small, env, gain, shift, out_bias, up_bias, down_bias):
    wide = plan.hidden // SMALL_ROWS
    at = SMALL_ROWS
    for layer in range(layers):
        second = at
        up = at + SMALL_ROWS
        first = 0 if layer == 0 else at + 2 * SMALL_ROWS
        at += (2 if layer == 0 else 3) * SMALL_ROWS
        gain[layer, 0:1, :] = small[first : first + 1, :]
        shift[layer, 0:1, :] = small[first + 1 : first + 2, :]
        gain[layer, 1:2, :] = small[second : second + 1, :]
        shift[layer, 1:2, :] = small[second + 1 : second + 2, :]
        out_bias[layer : layer + 1, :] = small[second + 2 : second + 3, :]
        down_bias[layer : layer + 1, :] = small[second + 3 : second + 4, :]
        for i in range(SMALL_ROWS):
            up_bias[layer : layer + 1, i * wide : (i + 1) * wide] = small[up + i : up + i + 1, 0:wide]
    env[...] = small[at : at + envs, :]


def emit_small(plan, layers, envs, small):
    shapes = [
        (envs, plan.width),
        (layers, 2, plan.width),
        (layers, 2, plan.width),
        (layers, plan.width),
        (layers, plan.hidden),
        (layers, plan.width),
    ]
    return pl.pallas_call(
        functools.partial(emit_small_kernel, plan, layers, envs),
        grid=(1,),
        in_specs=[full(small.shape)],
        out_specs=[full(s) for s in shapes],
        out_shape=[jax.ShapeDtypeStruct(s, F32) for s in shapes],
        compiler_params=params(8),
        cost_estimate=cost(1),
        name="emit_small",
    )(small)


def feed_grads_kernel(plan, me, lifted, before_low, low, hidden, keep, send, lifted_t, low_t):
    @pl.when(pl.program_id(0) == 0)
    def _():
        lifted_t[...] = lifted[...].T
        low_t[...] = low[...].T

    up = dot(lifted_t[...], before_low[...]).astype(BF16)
    down = dot(low_t[...], hidden[...]).astype(BF16)

    @pl.when(me[0] % 2 == 0)
    def _():
        keep[...] = up
        send[...] = down

    @pl.when(me[0] % 2 == 1)
    def _():
        keep[...] = down
        send[...] = up


def feed_grads(plan, me, lifted, before_low, low, hidden, away):
    block = (plan.block, plan.width)
    cols = plan.hidden // FF_STEPS
    wide = pl.BlockSpec((plan.block, cols), lambda j: (0, j))
    out = pl.BlockSpec((plan.width, cols), lambda j: (0, j))
    shape = result((plan.width, plan.hidden), BF16, True)
    return pl.pallas_call(
        functools.partial(feed_grads_kernel, plan),
        grid=(FF_STEPS,),
        in_specs=[pl.BlockSpec(memory_space=SMEM), full(block), wide, full(block), wide],
        out_specs=[out, out],
        out_shape=[shape, shape],
        scratch_shapes=[pltpu.VMEM((plan.width, plan.block), BF16)] * 2,
        compiler_params=params(16),
        cost_estimate=cost(5),
        name="feed_grads",
    )(me, *far([lifted], away), before_low, low, *far([hidden], away))


def head_grads_kernel(plan, kinds, beside, digit, *refs):
    me, refs = refs[0], refs[1:]
    scratch, refs = refs[-1], refs[:-1]
    columns = []
    for count in kinds:
        blocks, windows, refs = refs[:4], refs[4 : 4 + count], refs[4 + count :]
        place_blocks(plan, me, blocks, scratch)
        rights = [ref[i] for ref in windows for i in range(ref.shape[0])]
        total = None
        for slot, right in enumerate(rights):
            start = pl.multiple_of(plan.sequence(slot, me[0] // 2) * plan.stride, 16)
            part = dot(scratch[pl.ds(start, plan.window), :].T, right)
            total = part if total is None else total + part
        columns.append(total.astype(BF16))
    if beside:
        columns.append(refs[0][...])
        refs = refs[1:]
    value = jnp.concatenate(columns, axis=1) if len(columns) > 1 else columns[0]
    n = len(refs)
    if n == 1:
        refs[0][...] = value
        return
    count = plan.width // n
    for mine in range(n):

        @pl.when(digit[0] == mine)
        def _(mine=mine):
            for j, ref in enumerate(refs):
                at = (mine ^ j) * count
                ref[...] = value[at : at + count]


def head_grads(plan, me, digit, pieces, pairs, beside=()):
    cols = sum(p[1][0].shape[2] for p in pairs) + sum(b.shape[1] for b in beside)
    shape = (plan.width // pieces, cols)
    flat = [a for p in pairs for a in (*p[0], *p[1])] + list(beside)
    return pl.pallas_call(
        functools.partial(head_grads_kernel, plan, [len(p[1]) for p in pairs], len(beside)),
        grid=(1,),
        in_specs=[pl.BlockSpec(memory_space=SMEM)] * 2 + [full(a.shape) for a in flat],
        out_specs=[full(shape)] * pieces,
        out_shape=[jax.ShapeDtypeStruct(shape, BF16)] * pieces,
        scratch_shapes=[pltpu.VMEM((plan.total, plan.width), BF16)],
        compiler_params=params(20),
        cost_estimate=cost(5),
        name="head_grads",
    )(digit, me, *far(flat))


def swap(value, bit):
    size = lax.axis_size("head")
    return lax.ppermute(value, "head", [(i, i ^ bit) for i in range(size)])


def scatter(outs):
    to_diagonal, to_core, to_across, mine = outs
    first = swap(to_diagonal, 1)
    second = swap(to_core, 1)
    pair = (to_across.astype(F32) + first.astype(F32)).astype(BF16)
    return mine, second, swap(pair, 2)


def tie(*trees):
    return lax.optimization_barrier(trees)


class Bits:
    def __init__(self):
        self.heads = lax.axis_size("head")
        self.size = lax.axis_size("seq") * self.heads
        self.place = lax.axis_index("seq") * self.heads + lax.axis_index("head")
        self.place = self.place.astype(jnp.int32)
        seq = [self.heads << i for i in range((self.size // self.heads).bit_length() - 1)]
        self.core, self.across = (1, 1), (2, 2)
        self.seq = [(seq[0], seq[1]), (seq[1], seq[0])] + [(m, m) for m in seq[2:]]

    def bit(self, mask):
        return jnp.where((self.place & mask) > 0, 1, 0).astype(jnp.int32).reshape(1)

    def digit(self, step):
        core = self.place & 1
        value = jnp.int32(0)
        for i, (zero, one) in enumerate(step):
            mask = jnp.where(core == 0, zero, one)
            value = value + jnp.where((self.place & mask) > 0, 1 << i, 0)
        return value.astype(jnp.int32).reshape(1)

    def send(self, value, step, j):
        def partner(place):
            for i, masks in enumerate(step):
                if j >> i & 1:
                    place ^= masks[place & 1]
            return place

        pairs = [(p, partner(p)) for p in range(self.size)]
        return lax.ppermute(value, ("seq", "head"), pairs)


def cut(shape, pieces):
    if shape[0] % (16 * pieces) == 0:
        return 0
    if shape[1] % (LANES * pieces) == 0:
        return 1
    return None


def piece_at(shape, pieces, index):
    dim = cut(shape, pieces) if pieces > 1 else 0
    count = shape[dim] // pieces
    part = tuple(count if d == dim else shape[d] for d in range(2))
    if pieces == 1:
        return (slice(None), slice(None)), part
    window = pl.ds(pl.multiple_of(index * count, 16 if dim == 0 else LANES), count)
    return tuple(window if d == dim else slice(None) for d in range(2)), part


def fold_kernel(pieces, dim, digit, *refs):
    ins, outs = refs[: len(refs) - pieces], refs[len(refs) - pieces :]
    count = ins[0].shape[dim] // pieces
    for j, out in enumerate(outs):
        place = digit[0] ^ j if pieces > 1 else 0
        at = pl.ds(pl.multiple_of(place * count, LANES if dim else 16), count)
        where = (slice(None), at) if dim else (at, slice(None))
        total = ins[0][where].astype(F32)
        for ref in ins[1:]:
            total = total + ref[where].astype(F32)
        out[...] = total.astype(BF16)


def large(shape):
    return shape[0] * shape[1] >= 192 * 1024


def in_columns(shape, dim):
    return 1


def fold(digit, pieces, arrays):
    rows, cols = arrays[0].shape
    dim = cut((rows, cols), pieces)
    part = (rows, cols // pieces) if dim else (rows // pieces, cols)
    steps = in_columns((rows, cols), dim)
    of = lambda shape: pl.BlockSpec((shape[0], shape[1] // steps), lambda j: (0, j))
    return pl.pallas_call(
        functools.partial(fold_kernel, pieces, dim),
        grid=(steps,),
        in_specs=[pl.BlockSpec(memory_space=SMEM)] + [of((rows, cols))] * len(arrays),
        out_specs=[of(part)] * pieces,
        out_shape=[result(part, BF16, large(part))] * pieces,
        compiler_params=params(16),
        cost_estimate=cost(2 if large(arrays[0].shape) else 1),
        name="fold",
    )(digit, *far(arrays, large((rows, cols))))


def join_kernel(dim, digit, own, came, out):
    count = own.shape[dim]
    for j, ref in enumerate((own, came)):
        at = pl.ds(pl.multiple_of((digit[0] ^ j) * count, LANES if dim else 16), count)
        out[(slice(None), at) if dim else (at, slice(None))] = ref[...]


def join(digit, dim, own, came):
    rows, cols = own.shape
    whole = (rows, 2 * cols) if dim else (2 * rows, cols)
    steps = in_columns(whole, dim)
    of = lambda shape: pl.BlockSpec((shape[0], shape[1] // steps), lambda j: (0, j))
    return pl.pallas_call(
        functools.partial(join_kernel, dim),
        grid=(steps,),
        in_specs=[pl.BlockSpec(memory_space=SMEM), of((rows, cols)), of((rows, cols))],
        out_specs=of(whole),
        out_shape=result(whole, BF16, large(whole)),
        compiler_params=params(16),
        cost_estimate=cost(2 if large(whole) else 1),
        name="join",
    )(digit, *far((own, came), large((rows, cols))))


class Chain:
    def __init__(self, bits, plan, keep, send):
        self.bits, self.plan = bits, plan
        self.state = [keep, send]
        self.dims = [None]
        self.at = -1
        self.back = False
        self.done = False

    def work(self):
        bits, plan = self.bits, self.plan
        if not self.back:
            self.at += 1
            if self.at == 0:
                return
            if self.at == len(plan):
                self.at -= 1
                self.back = True
                (own,) = fold(bits.digit([plan[-1]]), 1, self.state)
                self.state = [own, own]
                return
            self.dims.append(cut(self.state[0].shape, 2))
            self.state = list(fold(bits.digit([plan[self.at]]), 2, self.state))
            return
        if self.at == 0:
            self.done = True
            return
        own = join(bits.digit([plan[self.at]]), self.dims[self.at], *self.state)
        self.at -= 1
        self.state = [own, own]

    def going(self):
        return self.state[:1] if self.back and not self.done else self.state

    def exchange(self):
        if not self.done:
            came = self.bits.send(self.state[1], [self.plan[self.at]], 1)
            self.state = [self.state[0], came]


def small_steps(bits):
    return [[b] for b in [bits.core, bits.across] + bits.seq]


def sum_small(bits, step, value):
    came = [bits.send(value, step, j) for j in range(1, 1 << len(step))]
    return functools.reduce(jnp.add, came, value)


def emit_feed_kernel(plan, count, me, digits, *refs):
    sources, (up, down, turned) = refs[: 2 * count], refs[-3:]
    size = plan.width // count
    own, other = sources[:count], sources[count:]
    for core, (ups, downs) in enumerate(((own, other), (other, own))):

        @pl.when(me[0] % 2 == core)
        def _(ups=ups, downs=downs):
            for j in range(count):
                rows = pl.ds(pl.multiple_of((digits[0] ^ j) * size, 16), size)
                up[rows, :] = ups[j][...].astype(F32)
                rows = pl.ds(pl.multiple_of((digits[1] ^ j) * size, 16), size)
                turned[rows, :] = downs[j][...]

    eye = jnp.where(
        lax.broadcasted_iota(jnp.int32, (plan.width, plan.width), 0)
        == lax.broadcasted_iota(jnp.int32, (plan.width, plan.width), 1),
        1.0,
        0.0,
    ).astype(BF16)
    down[...] = dot(turned[...], eye, TN)


def emit_feed(plan, me, digits, layer, layers, sources, before):
    cols = plan.hidden // FF_STEPS
    of = lambda a: pl.BlockSpec((a.shape[0], cols), lambda j: (0, j))
    anywhere = pl.BlockSpec(memory_space=pl.ANY)
    smem = pl.BlockSpec(memory_space=SMEM)

    def kernel(me_ref, digits_ref, *refs):
        ins, outs = refs[: len(sources)], refs[len(sources) + len(before) :]
        emit_feed_kernel(plan, len(sources) // 2, me_ref, digits_ref, *ins, *outs)

    return pl.pallas_call(
        kernel,
        grid=(FF_STEPS,),
        in_specs=[smem, smem] + [of(a) for a in sources] + [anywhere] * len(before),
        out_specs=[
            pl.BlockSpec((None, plan.width, cols), lambda j: (layer, 0, j)),
            pl.BlockSpec((None, cols, plan.width), lambda j: (layer, j, 0)),
        ],
        out_shape=[
            jax.ShapeDtypeStruct((layers, plan.width, plan.hidden), F32),
            jax.ShapeDtypeStruct((layers, plan.hidden, plan.width), F32),
        ],
        scratch_shapes=[pltpu.VMEM((plan.width, cols), BF16)],
        input_output_aliases={2 + len(sources) + i: i for i in range(len(before))},
        compiler_params=params(16),
        cost_estimate=cost(4),
        name="emit_feed",
    )(me, digits, *far(sources), *before)


def emit_heads_kernel(plan, layers, digit, *refs):
    sources, (into, out) = refs[:-2], refs[-2:]
    local = plan.local
    count = plan.width // len(sources)

    def put(ref, rows):
        for layer in range(layers):
            at = layer * 4 * local
            for t in range(3):
                into[layer, t, rows, :] = ref[:, at + t * local : at + (t + 1) * local].astype(F32)
            out[layer, :, rows] = ref[:, at + 3 * local : at + 4 * local].astype(F32).T

    if len(sources) == 1:
        put(sources[0], slice(0, count))
        return
    for mine in range(2):

        @pl.when(digit[0] == mine)
        def _(mine=mine):
            for j, ref in enumerate(sources):
                put(ref, slice((mine ^ j) * count, ((mine ^ j) + 1) * count))


def emit_heads(plan, digit, layers, sources):
    shapes = [(layers, 3, plan.width, plan.local), (layers, plan.local, plan.width)]
    return pl.pallas_call(
        functools.partial(emit_heads_kernel, plan, layers),
        grid=(1,),
        in_specs=[pl.BlockSpec(memory_space=SMEM)] + [full(a.shape) for a in sources],
        out_specs=[full(s) for s in shapes],
        out_shape=[jax.ShapeDtypeStruct(s, F32) for s in shapes],
        compiler_params=params(24),
        cost_estimate=cost(2),
        name="emit_heads",
    )(digit, *far(sources))


def body(
    tokens,
    actions,
    action_mask,
    frame_mask,
    environment_id,
    environment_embed,
    norm_gain,
    norm_bias,
    input_weight,
    output_weight,
    output_bias,
    up_weight,
    up_bias,
    down_weight,
    down_bias,
    cotangent,
):
    rows, width = tokens.shape
    seqs, frames, _ = actions.shape
    layers = input_weight.shape[0]
    envs = environment_embed.shape[0]
    plan = Plan(
        rows,
        lax.axis_size("head"),
        seqs,
        frames,
        width,
        input_weight.shape[3],
        up_weight.shape[2],
    )
    bits = Bits()
    me = lax.axis_index("head").astype(jnp.int32).reshape(1)
    as_rows = lambda t: t.reshape(layers, 1, -1)
    env_row = environment_id.reshape(1, seqs)
    stream, normed, *masks = prologue(
        plan,
        me,
        action_mask,
        frame_mask,
        env_row,
        tokens,
        actions,
        environment_embed,
        norm_gain,
        norm_bias,
    )
    own_slot, other_slots = [0], [1, 2]
    saved = []
    for layer in range(layers):
        away = False
        core, across = swap(normed, 1), swap(normed, 2)
        first = attend(plan, layer, own_slot, me, (normed, core), input_weight, masks, away)
        across, first = tie(across, first)
        blocks = (normed, core, across, swap(across, 1))
        *second, to_diagonal, to_core, to_across, mine = attend(
            plan,
            layer,
            other_slots,
            me,
            blocks,
            input_weight,
            masks,
            away,
            output_weight,
            first[1],
        )
        parts = scatter((to_diagonal, to_core, to_across, mine))
        middle, lifted, hidden, slope, *tail = forward_rest(
            plan,
            layer,
            layers,
            stream,
            parts,
            as_rows(output_bias),
            norm_gain,
            norm_bias,
            up_weight,
            as_rows(up_bias),
            down_weight,
            as_rows(down_bias),
        )
        saved.append((stream, blocks, first, second, middle, lifted, hidden, slope))
        if layer < layers - 1:
            stream, normed = tail
    mixed = tail[0]
    carry = jnp.pad(cotangent.astype(F32), ((0, plan.block - rows), (0, 0)))
    by_steps = len(bits.seq) == 3
    zero = jnp.zeros_like(me)
    stream, blocks, first, second, middle, lifted, hidden, slope = saved[-1]
    last = layers - 1

    def feed_back(layer, carry):
        stream, blocks, first, second, middle, lifted, hidden, slope = saved[layer]
        away = layer < last
        low, before_low, middle_grad, middle_low, second_sums, up_sums = back_rest(
            plan, layer, carry, middle, slope, norm_gain, up_weight, down_weight, away
        )
        core, across = swap(middle_low, 1), swap(middle_low, 2)
        by_chain = by_steps and layer == 0
        if layer == 0:
            own_grad = own_back(layer, middle_low, core)
            lifted, own_grad = tie(lifted, own_grad)
        else:
            lifted, core = tie(lifted, core)
            own_grad = None
        feed = feed_grads(
            plan, me if by_chain else zero, lifted, before_low, low, hidden, away
        )
        core, feed = tie(core, feed)
        return middle_grad, middle_low, core, across, own_grad, feed, second_sums, up_sums

    def own_back(layer, middle_low, core):
        return attend_back(
            plan,
            layer,
            [0],
            me,
            (middle_low, core),
            output_weight,
            masks,
            saved[layer][2],
            True,
        )[0]

    def start(chain, value):
        chain.state, value = tie(chain.state, value)
        chain.work()
        chain.state, value = tie(chain.state, value)
        chain.exchange()
        return value

    feed_plan = [bits.core] + bits.seq[:2] + [bits.across] + bits.seq[2:]
    held = {}

    def finish(state):
        middle_grad, middle_low, core, across, own_grad, last_sums = state
        heads, sums = {}, {}
        feed = None
        for layer in reversed(range(layers)):
            stream, blocks, first, second, middle, lifted, hidden, slope = saved[layer]
            tail = by_steps and layer == 0
            if layer < last:
                middle_grad, middle_low, core, across, own_grad, feed, *last_sums = feed_back(layer, carry)
                if tail:
                    feed = Chain(bits, feed_plan, *feed)
                    across = start(feed, across)
            else:
                across, own_grad = tie(across, own_grad)
            middle_blocks = (middle_low, core, across, swap(across, 1))
            if tail:
                middle_blocks = start(feed, middle_blocks)
            both_grad, *outs = attend_back(
                plan,
                layer,
                [1, 2],
                me,
                middle_blocks,
                output_weight,
                masks,
                second,
                True,
                input_weight,
                (own_grad,),
            )
            if tail:
                outs, feed.state = tie(outs, feed.state)
            to_diagonal, to_core, to_across, mine = outs
            from_diagonal = swap(to_diagonal, 1)
            from_core = swap(to_core, 1)
            pair = (to_across.astype(F32) + from_diagonal.astype(F32)).astype(BF16)
            pair_came = swap(pair, 2)
            if tail:
                feed.work()
                blocks, feed.state = tie(blocks, feed.state)
                feed.exchange()
            out_pair = (middle_blocks, (first[1], second[1]))
            parts = (mine, from_core, pair_came)
            if tail:
                parts, feed.state = tie(parts, feed.state)
            else:
                in_pair = (blocks, (own_grad, both_grad))
                (heads[layer],) = head_grads(plan, me, zero, 1, (in_pair, out_pair))
                parts, heads[layer] = tie(parts, heads[layer])
            carry, sums[layer] = carry_back(
                plan,
                layer,
                me,
                env_row,
                envs,
                parts,
                stream,
                middle_grad,
                norm_gain,
                [] if layer else [*last_sums] + [s for l in range(1, layers) for s in sums[l]],
                True,
            )
            if tail:
                sums[layer] = start(feed, sums[layer])
                blocks, sums[layer] = tie(blocks, sums[layer])
                in_pair = (blocks, (own_grad, both_grad))
                digit = bits.digit([bits.seq[0]])
                halves = head_grads(
                    plan, me, digit, 2, (in_pair, out_pair), [heads[l] for l in range(1, layers)]
                )
                halves, feed.state = tie(halves, feed.state)
                heads = Chain(bits, bits.seq, *halves)
            if layer:
                sums[layer] = (*last_sums, sums[layer])
        small = sums[0]
        if by_steps:
            for step in small_steps(bits)[:CUT]:
                small = start(feed, small)
                small = start(heads, small)
                small = sum_small(bits, step, small)
            for chain in (feed, heads):
                chain.state, small = tie(chain.state, small)
                chain.work()
            held["chains"] = [feed, heads]
            return carry, small, [feed.going(), heads.going()]
        small, feed = lax.psum((small, feed), ("seq", "head"))
        heads = lax.psum(jnp.concatenate([heads[l] for l in range(layers)], axis=1), "seq")
        return carry, small, [list(feed), [heads]]

    assert layers == 2
    middle_grad, middle_low, core, across, _, feed, *last_sums = feed_back(last, carry)
    feed_total = lax.psum(feed, ("seq", "head"))
    own_grad = own_back(last, middle_low, core)
    across, own_grad = tie(across, own_grad)
    state = (middle_grad, middle_low, core, across, own_grad, tuple(last_sums))
    shapes = jax.eval_shape(finish, state)
    carry, small, states = lax.cond(
        frame_mask[0, 0, 0] > 0,
        finish,
        lambda _: jax.tree.map(lambda s: jnp.zeros(s.shape, s.dtype), shapes),
        state,
    )
    states, small, feed_total = tie(states, small, feed_total)
    two = jnp.zeros((2,), jnp.int32)
    if by_steps:
        feed, heads = held["chains"]
        for chain, state in zip((feed, heads), states):
            chain.state = list(state) * (3 - len(state))
        rest = small_steps(bits)[CUT:]
        assert feed.at == 1
        mine = feed.state[0]
        came = bits.send(mine, [feed_plan[1]], 1)
        from_core = bits.send(mine, [bits.core], 1)
        heads.exchange()
        for step in rest:
            small = sum_small(bits, step, small)
        filled = emit_feed(plan, zero, two, last, layers, feed_total, ())
        came, filled, small = tie(came, filled, small)
        also_core = bits.send(came, [bits.core], 1)
        while not heads.done:
            heads.work()
            heads.exchange()
        digits = jnp.concatenate([bits.bit(mask) for mask in feed_plan[1]])
        sources = [mine, came, from_core, also_core]
        feed_out = emit_feed(plan, me, digits, 0, layers, sources, filled)
        digit = bits.digit([bits.seq[0]])
        heads, feed_out = tie(heads.state, feed_out)
    else:
        filled = emit_feed(plan, zero, two, last, layers, feed_total, ())
        feed, heads = states
        feed_out = emit_feed(plan, zero, two, 0, layers, feed, filled)
        digit = zero
    head_out = emit_heads(plan, digit, layers, heads)
    environment_total, gain_out, shift_out, out_bias_out, up_bias_out, down_bias_out = emit_small(
        plan, layers, envs, small
    )
    return (
        mixed,
        carry,
        environment_total,
        gain_out,
        shift_out,
        head_out[0],
        head_out[1],
        out_bias_out,
        feed_out[0],
        up_bias_out,
        feed_out[1],
        down_bias_out,
    )


def solution(mesh):
    return jax.shard_map(
        body,
        mesh=mesh,
        in_specs=(
            P(("seq", "head"), None),
            P("seq", None, None),
            P("seq", None),
            P("seq", None, None),
            P("seq"),
            P(),
            P(),
            P(),
            P(None, None, None, "head"),
            P(None, "head", None),
            P(),
            P(),
            P(),
            P(),
            P(),
            P(("seq", "head"), None),
        ),
        out_specs=(
            P(("seq", "head"), None),
            P(("seq", "head"), None),
            P(),
            P(),
            P(),
            P(None, None, None, "head"),
            P(None, "head", None),
            P(),
            P(),
            P(),
            P(),
            P(),
        ),
        check_vma=False,
    )
```
